32 devices in a mesh: ship: 8 (over z, y), boot: 4 (over x, core).
Axes of the slice: x: 2, y: 2, z: 4, core: 2. Of those that a mesh axis runs over, the one named last changes fastest.
Arguments:
- fitted: float32 [131072], P('ship'), may hold values from -6 to 6
- resid: float32 [131072], P('ship'), may hold values from -32 to 32
- row_weight: float32 [131072], P('ship'), may hold values from 0.5 to 2
- lane_block: int32 [131072, 1], P('ship'), may hold values from 0 to 7; in each aligned block of 16384 rows (0 to 16383, 16384 to 32767, ...) at most 4096 rows name the same one
- lane_within: int32 [131072], P('ship'), may hold values from 0 to 2047
- week_id: int32 [131072], P('ship'), may hold values from 0 to 259
- supplier_runs: int32 [8, 128], P('ship'), may hold values from 1 to 512, 16384 in all within a row
- signs: int32 [128, 1024], P('boot', 'ship'), may hold values from 0 to 1
- supplier_scale: float32 [1024], P('ship'), may hold values from 0.17677669 to 0.70710677
- lane_scale: float32 [16384], P('ship'), may hold values from 0.70710677 to 2.828427
- week_scale: float32 [260], replicated, may hold values from 0.089076206 to 0.35630482
Outputs:
- v_supplier: float32 [128, 1024], P('boot', 'ship')
- v_lane: float32 [128, 16384], P('boot', 'ship')
- v_week: float32 [128, 260], P('boot')
- u_next: float32 [128, 131072], P('boot', 'ship')
- step_size: float32 [128], P('boot')
- spread_supplier: float32 [1024], P('ship')
- spread_lane: float32 [16384], P('ship')
The draws below stay inside these ranges and needn't reach their ends.
Inputs may be any that keep to these rules, and one draw needn't show every extreme that they name: `lane_block`: among the 16384 shipments of one device at most 4096 have the same lane block, and in every draw some device has exactly 4096 in some block. `supplier_runs`: each row sums to 16384; in every row one supplier has exactly the largest count.
All inputs are finite; a program needn't handle non-finite values.
Results may differ from the reference program's by a relative error of at most 0.00011.
Values sent between devices are 32-bit elements; how exact they have to be, the bound alone decides.
No kernel may reach another device: no remote copies, remote signals or barrier semaphores. Data moves between devices by JAX's collectives and lax.ppermute only.
A program may use at most 64 MiB of HBM per device.

```python
import math
import jax
import jax.numpy as jnp
import numpy as np
from jax import lax

ROWS = 16384
S_DEV = 128
LANES = 16384
WEEKS = 260
SHIPMENTS = 131072
SUPPLIERS = 1024
COLS = 128
L_DEV = 2048
CAP = 4096
EFFECTS = 17668
N_SHIP = 8


def draw_resid(key, part):
    key = jax.random.fold_in(key, 11)
    first, second = jax.random.split(key)
    place = jnp.arange(SHIPMENTS, dtype=jnp.float32) / SHIPMENTS
    rough = jnp.exp(jax.random.uniform(second, (SHIPMENTS,), jnp.float32, math.log(0.5), math.log(2.0)))
    base = jnp.clip(jax.random.normal(first, (SHIPMENTS,), jnp.float32), -4.0, 4.0)
    rise = jnp.exp(place * math.log(3.0))
    return base * rough * rise


def set_ends(entries, own_key, least, high):
    spot = [jax.random.randint(jax.random.fold_in(own_key, axis), (), 0, length) for axis, length in enumerate(entries.shape)]
    longest = entries.shape.index(max(entries.shape))
    next_to = spot[:longest] + [(spot[longest] + 1) % entries.shape[longest]] + spot[longest + 1:]
    return entries.at[tuple(spot)].set(least).at[tuple(next_to)].set(high)


def shard_levels(key, dims, cuts, least, high):
    level, own = 1.0, jax.random.fold_in(key, 6)
    for axis_at, parts in cuts:
        draws = jnp.exp(jax.random.uniform(jax.random.fold_in(own, axis_at), (parts,), jnp.float32, least / len(cuts), high / len(cuts)))
        level = level * jnp.repeat(draws, dims[axis_at] // parts).reshape([-1 if axis == axis_at else 1 for axis in range(len(dims))])
    return level


def split_up(number_of, total, most, slope):
    weights = [(1 << 20) // math.isqrt(grade ** slope) + 1 for grade in range(2, number_of + 1)]
    rest, counts = total - most - (number_of - 1), [1] * (number_of - 1)
    while rest > 0:
        free = [i for i in range(number_of - 1) if counts[i] < most]
        mass, remaining = sum([weights[i] for i in free]), rest
        for i in free:
            more = min(most - counts[i], max(1, remaining * weights[i] // mass), rest)
            counts[i] = counts[i] + more
            rest = rest - more
    return np.array([most] + counts)


def ragged_sizes(own_key, count, total, limit, skew):
    if count == 2:
        one = jax.random.randint(own_key, (), max(1, total - limit), min(limit, total - 1) + 1)
        return jnp.stack([one, total - one])
    tallies = jnp.asarray(split_up(count, total, limit, skew), jnp.int32)
    couples = (count - 1) // 2
    source_of, taker = tallies[1:1 + 2 * couples:2], tallies[2:2 + 2 * couples:2]
    slack = jnp.minimum(source_of - 1, limit - taker)
    shifted = jax.random.randint(jax.random.fold_in(own_key, 1), (couples,), 0, 1 << 20) % (slack + 1)
    tallies = tallies.at[1:1 + 2 * couples:2].set(source_of - shifted).at[2:2 + 2 * couples:2].set(taker + shifted)
    return tallies[jax.random.permutation(jax.random.fold_in(own_key, 2), count)]


def deal_out(own_key, own, number, rows, amount, top, limit, slope):
    order = jax.random.permutation(own_key, amount)
    packed, common = load_shares(amount, rows * top, limit, slope, True), load_shares(amount, rows * top, limit, slope, False)
    places = jnp.arange(amount)

    def named(lengths, offset_by):
        used = int((lengths > 0).sum())
        fixed = max(1, used // 4)
        shifted = fixed + (places - fixed + offset_by * (used - fixed)) % max(1, amount - fixed)
        return jnp.zeros((amount,), jnp.int32).at[order[jnp.where(places < fixed, places, shifted)]].set(jnp.asarray(lengths, jnp.int32))

    lengths = jnp.where(number % 4 == 0, named(packed, number // 4), named(common, number - number // 4 - 1))
    mixed = jax.random.permutation(jax.random.fold_in(own, 3), amount)
    source_of, taker = mixed[0:amount // 2 * 2:2], mixed[1:amount // 2 * 2:2]
    slack = jnp.minimum(lengths[source_of] - 1, limit - lengths[taker]) // 2
    slack = jnp.where((source_of == order[0]) | (taker == order[0]) | (lengths[taker] == 0), 0, jnp.maximum(slack, 0))
    shifted = jax.random.randint(jax.random.fold_in(own, 4), (amount // 2,), 0, 1 << 20) % (slack + 1)
    lengths = lengths.at[source_of].add(-shifted).at[taker].add(shifted)
    members = jnp.searchsorted(jnp.cumsum(lengths), jnp.arange(rows * top), side="right").astype(jnp.int32)
    grid = members.reshape(top, rows).T
    grid = grid[jax.random.permutation(jax.random.fold_in(own, 1), rows)]
    offset_by = jax.random.randint(jax.random.fold_in(own, 2), (rows, 1), 0, top)
    return jnp.take_along_axis(grid, (jnp.arange(top)[None, :] + offset_by) % top, axis=1)


def load_shares(count, total, bound, slope, full):
    loads = [(1 << 20) // math.isqrt(grade ** slope) + 1 for grade in range(1, count + 1)]
    largest = bound if full else min(bound, max(-(-total // count), total * loads[0] // sum(loads)))
    least = 1 if total - largest >= count - 1 else 0
    counts, rest = [largest] + [least] * (count - 1), total - largest - least * (count - 1)
    while rest > 0:
        candidates = [i for i in range(1, count) if counts[i] < largest] or [i for i in range(1, count) if counts[i] < bound]
        pool, left = sum([loads[i] for i in candidates]), rest
        for i in candidates:
            extra = min(bound - counts[i], max(1, left * loads[i] // pool), rest)
            counts[i] = counts[i] + extra
            rest = rest - extra
    return np.array(counts)


def bell_draw(key, shape, deviation, limit, pieces=(), kind=jnp.bfloat16):
    result = deviation * jax.random.normal(key, shape, jnp.float32)
    if pieces:
        result = result * shard_levels(key, shape, pieces, -0.22, 0.18)
    return jnp.clip(result, -limit, limit).astype(kind)


def setup_inputs(seed: int = 0) -> dict:
    splits = jax.random.split(jax.random.key(seed), 12)
    fitted = bell_draw(splits[0], (SHIPMENTS,), 1.0, 6.0, ((0, 8),), jnp.float32)
    resid = draw_resid(jax.random.fold_in(splits[11], 71), 0)
    row_weight = jnp.clip(jnp.exp(math.log(2.0) - 1.3862944 * jax.random.uniform(splits[2], (SHIPMENTS,), jnp.float32) ** shard_levels(splits[2], (SHIPMENTS,), ((0, 8),), -0.2, 0.2)), 0.5, 2.0)
    lane_block_keys = jax.random.split(jax.random.fold_in(splits[3], 1), SHIPMENTS // ROWS)
    lane_block_turns = jax.random.permutation(jax.random.fold_in(splits[3], 3), SHIPMENTS // ROWS)
    lane_block = jax.vmap(lambda own, number: deal_out(jax.random.fold_in(splits[3], 2), own, number, ROWS, N_SHIP, 1, CAP, 2))(lane_block_keys, lane_block_turns).reshape((SHIPMENTS, 1))
    lane_within = set_ends(jax.random.randint(splits[4], (SHIPMENTS,), 0, L_DEV), jax.random.fold_in(splits[4], 1), 0, L_DEV - 1).astype(jnp.int32)
    week_id = set_ends(jax.random.randint(splits[5], (SHIPMENTS,), 0, WEEKS), jax.random.fold_in(splits[5], 1), 0, WEEKS - 1).astype(jnp.int32)
    supplier_runs = jax.vmap(lambda own: ragged_sizes(own, S_DEV, ROWS, 4 * ROWS // S_DEV, 2))(jax.random.split(splits[6], N_SHIP)).reshape((N_SHIP, S_DEV)).astype(jnp.int32)
    signs = set_ends(jax.random.randint(splits[7], (COLS, SUPPLIERS), 0, 2), jax.random.fold_in(splits[7], 1), 0, 1).astype(jnp.int32)
    supplier_scale = jnp.clip(jnp.exp(math.log(0.70710677) - 1.3862944 * jax.random.uniform(splits[8], (SUPPLIERS,), jnp.float32) ** shard_levels(splits[8], (SUPPLIERS,), ((0, 8),), -0.2, 0.2)), 0.17677669, 0.70710677)
    lane_scale = jnp.clip(jnp.exp(math.log(2.828427) - 1.3862944 * jax.random.uniform(splits[9], (LANES,), jnp.float32) ** shard_levels(splits[9], (LANES,), ((0, 8),), -0.2, 0.2)), 0.70710677, 2.828427)
    week_scale = jnp.clip(jnp.exp(jax.random.uniform(splits[10], (WEEKS,), jnp.float32, math.log(0.089076206), math.log(0.35630482))), 0.089076206, 0.35630482)
    return dict(fitted=fitted, resid=resid, row_weight=row_weight, lane_block=lane_block, lane_within=lane_within, week_id=week_id, supplier_runs=supplier_runs, signs=signs, supplier_scale=supplier_scale, lane_scale=lane_scale, week_scale=week_scale)


EPS = 1e-06

def lane_sums(values, ids, count):
    return jax.ops.segment_sum(values.T, ids, count).T

def reference(fitted, resid, row_weight, lane_block, lane_within, week_id, supplier_runs, signs, supplier_scale, lane_scale, week_scale):
    supplier = jnp.repeat(jnp.arange(SUPPLIERS, dtype=jnp.int32), supplier_runs.reshape(-1), total_repeat_length=SHIPMENTS)
    lane = (lane_block[:, 0] * L_DEV + lane_within).astype(jnp.int32)
    ratio = EFFECTS / SHIPMENTS
    sign_value = (2 * signs - 1).astype(jnp.float32)
    rhs = fitted[None, :] + sign_value[:, supplier] * resid[None, :]
    beta_first = jnp.sqrt(lax.optimization_barrier(jnp.sum(rhs * rhs, axis=1)) / SHIPMENTS + EPS)
    basis = rhs / beta_first[:, None]
    weighted = basis * row_weight[None, :]
    p_supplier = ratio * supplier_scale[None, :] * lane_sums(weighted, supplier, SUPPLIERS)
    p_lane = ratio * lane_scale[None, :] * lane_sums(weighted, lane, LANES)
    p_week = ratio * week_scale[None, :] * lane_sums(weighted, week_id, WEEKS)
    total = lax.optimization_barrier(jnp.sum(p_supplier * p_supplier, axis=1)) + lax.optimization_barrier(jnp.sum(p_lane * p_lane, axis=1)) + lax.optimization_barrier(jnp.sum(p_week * p_week, axis=1))
    alpha = jnp.sqrt(total / EFFECTS + EPS)
    v_supplier = p_supplier / alpha[:, None]
    v_lane = p_lane / alpha[:, None]
    v_week = p_week / alpha[:, None]
    forward = (v_supplier * supplier_scale[None, :])[:, supplier]
    forward = forward + (v_lane * lane_scale[None, :])[:, lane]
    forward = forward + (v_week * week_scale[None, :])[:, week_id]
    residual = row_weight[None, :] * forward - alpha[:, None] * basis
    beta_next = jnp.sqrt(lax.optimization_barrier(jnp.sum(residual * residual, axis=1)) / SHIPMENTS + EPS)
    u_next = residual / beta_next[:, None]
    step_size = alpha * beta_first / (alpha * alpha + beta_next * beta_next)
    x_supplier = step_size[:, None] * v_supplier
    x_lane = step_size[:, None] * v_lane
    spread_supplier = jnp.sqrt(lax.optimization_barrier(jnp.sum(x_supplier * x_supplier, axis=0)) / COLS + EPS)
    spread_lane = jnp.sqrt(lax.optimization_barrier(jnp.sum(x_lane * x_lane, axis=0)) / COLS + EPS)
    return (v_supplier, v_lane, v_week, u_next, step_size, spread_supplier, spread_lane)
```

```python
import functools

import jax
import jax.numpy as jnp
from jax import lax
from jax.experimental import pallas as pl
from jax.experimental.pallas import tpu as pltpu
from jax.sharding import PartitionSpec as P

EPS = 1e-06
BLOCK = 256
SLOTS = 7
LANES_WIDE = 128
VMEM = pl.BlockSpec(memory_space=pltpu.VMEM)
SMEM = pl.BlockSpec(memory_space=pltpu.SMEM)
PARAMS = pltpu.CompilerParams(vmem_limit_bytes=40 << 20)


def split(value):
    high = value.astype(jnp.bfloat16)
    low = (value - high.astype(jnp.float32)).astype(jnp.bfloat16)
    return high, low


def product(left, right):
    return jnp.dot(left, right, precision=lax.Precision.HIGHEST, preferred_element_type=jnp.float32)


def product_rows(left, hot):
    return lax.dot_general(
        left,
        hot,
        (((1,), (1,)), ((), ())),
        precision=lax.Precision.HIGHEST,
        preferred_element_type=jnp.float32,
    )


def swap(value, axis, step):
    size = lax.axis_size(axis)
    return lax.ppermute(value, axis, [(i, i ^ step) for i in range(size)])


def sum_over(value, axis):
    step = 1
    while step < lax.axis_size(axis):
        value = value + swap(value, axis, step)
        step *= 2
    return value


def lane_sums_kernel(low_n, turn_n, with_prev, meta, planes, signs, *refs):
    if with_prev:
        prev, outs, acc, acc_fit = refs[:turn_n], refs[turn_n : 2 * turn_n], refs[-2], refs[-1]
    else:
        prev, outs, acc, acc_fit = None, refs[:turn_n], refs[-2], refs[-1]
    suppliers = signs.shape[1]
    columns = outs[0].shape[0]
    own = outs[0].shape[1]
    rows = (planes.shape[0] - 8) // 3
    blocks = rows * 128 // BLOCK
    offset, turn = meta[2, 0], meta[2, 1]
    shift = low_n.bit_length() - 1
    acc[...] = jnp.zeros_like(acc)
    acc_fit[...] = jnp.zeros_like(acc_fit)
    high_at = lax.broadcasted_iota(jnp.int32, (8, BLOCK), 0)
    place = lax.broadcasted_iota(jnp.int32, (8, BLOCK), 1)
    low_at = lax.broadcasted_iota(jnp.int32, (low_n, BLOCK), 0)

    def two_rows(start):
        pair = [planes[pl.ds(start + u, 1), :] for u in range(BLOCK // 128)]
        return jnp.concatenate(pair, axis=1)

    def prepare(block):
        row = block * (BLOCK // 128)
        local = two_rows(row).astype(jnp.int32) - offset
        high, low = local >> shift, local & (low_n - 1)
        match = jnp.broadcast_to(high, (8, BLOCK)) == high_at
        fit = jnp.where(match, jnp.broadcast_to(two_rows(rows + row), (8, BLOCK)), 0.0)
        res = jnp.where(match, jnp.broadcast_to(two_rows(2 * rows + row), (8, BLOCK)), 0.0)
        hot = jnp.where(jnp.broadcast_to(low, (low_n, BLOCK)) == low_at, 1.0, 0.0).astype(jnp.bfloat16)
        return fit, res, hot

    def group(first, block, fit, res, hot):
        at = place + block * BLOCK
        parts = []
        for u in range(SLOTS):
            inside = (at >= meta[0, first + u]) & (at < meta[0, first + u + 1])
            parts.append(jnp.where(inside, res, 0.0))
        left = jnp.concatenate(parts + [fit], axis=0)
        both = lax.dot_general(
            jnp.concatenate(split(left), axis=0),
            hot,
            (((1,), (1,)), ((), ())),
            preferred_element_type=jnp.float32,
        )
        return both[: 8 * SLOTS + 8] + both[8 * SLOTS + 8 :]

    def add(first, sums):
        at = pl.ds(pl.multiple_of(first * 8, 8), 8 * SLOTS)
        for u in range(low_n // 128):
            acc[u, at, :] = acc[u, at, :] + sums[: 8 * SLOTS, u * 128 : (u + 1) * 128]

    unroll = 4

    @pl.loop(0, blocks // unroll)
    def _(step):
        ready = [prepare(step * unroll + u) for u in range(unroll)]
        firsts = [meta[1, step * unroll + u] for u in range(unroll)]
        sums = [group(firsts[u], step * unroll + u, *ready[u]) for u in range(unroll)]
        for u in range(unroll):
            add(firsts[u], sums[u])
        acc_fit[...] = acc_fit[...] + sum(one[8 * SLOTS :] for one in sums)
        for u in range(unroll):
            block = step * unroll + u
            more = (meta[1, block + 1] - firsts[u]) // SLOTS

            @pl.loop(0, more)
            def _(turn_at):
                first = firsts[u] + (turn_at + 1) * SLOTS
                fit, res, hot = prepare(block)
                add(first, group(first, block, fit, res, hot))

    for part in range(turn_n):
        here = pl.multiple_of((turn ^ part) * columns, columns)
        sign = (2 * signs[pl.ds(here, columns), :] - 1).astype(jnp.float32).astype(jnp.bfloat16)
        left = jnp.concatenate([sign, sign], axis=1)
        for high in range(-(-own // low_n)):
            rows_at = pl.ds(high, suppliers, stride=8)
            wide = jnp.concatenate([acc[u, rows_at, :] for u in range(low_n // 128)], axis=1)
            right = jnp.concatenate(split(wide), axis=0)
            total = jnp.dot(left, right, preferred_element_type=jnp.float32)
            total = total + jnp.broadcast_to(acc_fit[high : high + 1, :], total.shape)
            at = slice(high * low_n, (high + 1) * low_n)
            if with_prev:
                total = total + prev[part][:, at]
            outs[part][:, at] = total


def lane_sums(meta, planes, signs, prev, columns, own, turn_n):
    low_n = max(own // 8, 128)
    suppliers = signs.shape[1]
    shape = jax.ShapeDtypeStruct((columns, own), jnp.float32)
    return pl.pallas_call(
        functools.partial(lane_sums_kernel, low_n, turn_n, bool(prev)),
        out_shape=[shape] * turn_n,
        in_specs=[SMEM, VMEM, VMEM] + [VMEM] * len(prev),
        out_specs=[VMEM] * turn_n,
        scratch_shapes=[
            pltpu.VMEM((low_n // 128, (suppliers + SLOTS + 1) * 8, 128), jnp.float32),
            pltpu.VMEM((8, low_n), jnp.float32),
        ],
        compiler_params=PARAMS,
        name="lane_sums",
    )(meta, planes, signs, *prev)


def table_kernel(ratio, scale, *refs):
    parts, entries, table, squares = refs[:-3], refs[-3], refs[-2], refs[-1]
    total = parts[0][...]
    for part in parts[1:]:
        total = total + part[...]
    by = jnp.broadcast_to(scale[...], total.shape)
    entry = ratio * by * total
    entries[...] = entry
    squares[...] = jnp.sum(entry * entry, axis=1, keepdims=True)
    scaled = by * entry
    quarter = table.shape[0]
    count = total.shape[1] // quarter
    stacked = jnp.concatenate([scaled[:, u * quarter : (u + 1) * quarter] for u in range(count)], axis=0)
    table[...] = stacked.T


def lane_table(ratio, scale, parts):
    columns, own = parts[0].shape
    quarter = own * columns // LANES_WIDE
    return pl.pallas_call(
        functools.partial(table_kernel, ratio),
        out_shape=[
            jax.ShapeDtypeStruct((columns, own), jnp.float32),
            jax.ShapeDtypeStruct((quarter, LANES_WIDE), jnp.float32),
            jax.ShapeDtypeStruct((columns, 1), jnp.float32),
        ],
        in_specs=[VMEM] * (1 + len(parts)),
        out_specs=[VMEM] * 3,
        compiler_params=PARAMS,
        name="lane_table",
    )(scale, *parts)


def forward_kernel(index, lane_part, weight, inverse, base, *refs):
    tables, out, squares, table, first, second, total = refs[:-6], *refs[-6:]
    at = 0
    for piece in tables:
        table[at : at + piece.shape[0], :] = piece[...]
        at += piece.shape[0]
    groups = weight.shape[0]
    columns = out.shape[0]
    scale = jnp.broadcast_to(inverse[...], (columns, 128))
    total[...] = jnp.zeros_like(total)

    def gather(group, store):
        for u in range(128):
            store[u : u + 1, :] = table[pl.ds(index[group * 128 + u], 1), :]

    def finish(group, store):
        turned = store[...].T
        part = jnp.broadcast_to(lane_part[pl.ds(group, 1), :], (columns, 128))
        picked = turned[0:columns]
        for u in range(1, 128 // columns):
            picked = jnp.where(part == u, turned[u * columns : (u + 1) * columns], picked)
        at = pl.ds(pl.multiple_of(group * 128, 128), 128)
        by = jnp.broadcast_to(weight[pl.ds(group, 1), :], (columns, 128))
        value = base[:, at] + picked * by * scale
        out[:, at] = value
        total[...] = total[...] + value * value

    gather(0, first)

    @pl.loop(0, groups // 2)
    def _(step):
        gather(2 * step + 1, second)
        finish(2 * step, first)
        gather(jnp.minimum(2 * step + 2, groups - 1), first)
        finish(2 * step + 1, second)

    squares[...] = jnp.sum(total[...], axis=1, keepdims=True)


def forward_lanes(index, lane_part, weight, inverse, base, tables):
    columns, rows = base.shape
    lines = sum(piece.shape[0] for piece in tables)
    return pl.pallas_call(
        forward_kernel,
        out_shape=[
            jax.ShapeDtypeStruct((columns, rows), jnp.float32),
            jax.ShapeDtypeStruct((columns, 1), jnp.float32),
        ],
        in_specs=[SMEM] + [VMEM] * (4 + len(tables)),
        out_specs=[VMEM] * 2,
        scratch_shapes=[
            pltpu.VMEM((lines, LANES_WIDE), jnp.float32),
            pltpu.VMEM((128, LANES_WIDE), jnp.float32),
            pltpu.VMEM((128, LANES_WIDE), jnp.float32),
            pltpu.VMEM((columns, 128), jnp.float32),
        ],
        compiler_params=PARAMS,
        name="forward_lanes",
    )(index, lane_part, weight, inverse, base, *tables)


def gather_tables(table, n_ship):
    if n_ship > 16:
        return [lax.all_gather(table, "ship", axis=0, tiled=True)], False
    held = {0: table}
    for step in range(2, n_ship, 2):
        held[step] = swap(table, "ship", step)
    for step in range(0, n_ship, 2):
        held[step + 1] = swap(held[step], "ship", 1)
    return [held[step] for step in range(n_ship)], True


def on_device(
    fitted,
    resid,
    row_weight,
    lane_block,
    lane_within,
    week_id,
    supplier_runs,
    signs,
    supplier_scale,
    lane_scale,
    week_scale,
):
    rows = fitted.shape[0]
    columns = signs.shape[0]
    n_ship = lax.axis_size("ship")
    n_boot = lax.axis_size("boot")
    me_ship = lax.axis_index("ship")
    me_boot = lax.axis_index("boot")
    lane_own = lane_scale.shape[0]
    weeks = week_scale.shape[0]
    supplier_own = supplier_scale.shape[0]
    shipments_all = rows * n_ship
    effects_all = supplier_own * n_ship + lane_own * n_ship + weeks
    ratio = effects_all / shipments_all
    share = n_ship // n_boot

    owner = lane_block[:, 0]
    lane = owner * lane_own + lane_within
    runs = supplier_runs[0]
    before = jnp.arange(supplier_own)
    run_end = jnp.sum(jnp.where(before[None, :] <= before[:, None], runs[None, :], 0), axis=1)
    first_of = jnp.sum(
        (run_end[None, :] <= (jnp.arange(128, dtype=jnp.int32) * BLOCK)[:, None]).astype(jnp.int32), axis=1
    )
    square = (rows // 128, 128)
    planes = jnp.concatenate(
        [
            lane.astype(jnp.float32).reshape(square),
            (row_weight * fitted).reshape(square),
            (row_weight * resid).reshape(square),
            run_end.astype(jnp.float32)[None, :],
            first_of.astype(jnp.float32)[None, :],
            jnp.zeros((6, 128), jnp.float32),
        ],
        axis=0,
    )
    all_signs = lax.all_to_all(jnp.broadcast_to(signs[None], (n_boot,) + signs.shape), "boot", 0, 0)
    all_signs = all_signs.reshape(n_boot * columns, supplier_own)
    sums = []
    for turn in range(share):
        pairs = []
        for a in range(n_boot):
            for r in range(share):
                for b in range(n_boot):
                    pairs.append(((a * share + r) * n_boot + b, (b * share + (r + turn) % share) * n_boot + a))
        got = lax.ppermute(planes, ("ship", "boot"), pairs)
        got_signs = lax.ppermute(all_signs, ("ship", "boot"), pairs)
        start = got[3 * square[0]].astype(jnp.int32)
        firsts = got[3 * square[0] + 1].astype(jnp.int32)
        pad = supplier_own + 128
        start = jnp.concatenate([jnp.zeros((1,), jnp.int32), start, jnp.full((127,), rows, jnp.int32)])
        firsts = jnp.concatenate([firsts, jnp.zeros((pad - 128,), jnp.int32)])
        place = jnp.concatenate(
            [(me_ship * lane_own)[None], me_boot[None], jnp.zeros((pad - 2,), jnp.int32)]
        ).astype(jnp.int32)
        sums = lane_sums(jnp.stack([start, firsts, place]), got, got_signs, sums, columns, lane_own, n_boot)
    parts = [sums[0]] + [swap(sums[step], "boot", step) for step in range(1, n_boot)]
    entry, table, entry_square = lane_table(ratio, lane_scale[None, :], parts)
    tables, by_step = gather_tables(table, n_ship)

    position = jnp.arange(rows, dtype=jnp.int32)
    run_start = run_end - runs
    supplier_hot = (
        (position[:, None] >= run_start[None, :]) & (position[:, None] < run_end[None, :])
    ).astype(jnp.float32)
    week_hot = (week_id[:, None] == jnp.arange(weeks, dtype=jnp.int32)[None, :]).astype(jnp.float32)
    sign_value = (2 * signs - 1).astype(jnp.float32)
    rhs = fitted[None, :] + product_rows(sign_value, supplier_hot) * resid[None, :]
    square_sum = jnp.sum(rhs * rhs, axis=1)
    weighted = rhs * row_weight[None, :]
    week_part = product(weighted, week_hot)
    supplier_part = product(weighted, supplier_hot)
    early = sum_over(jnp.concatenate([week_part, square_sum[:, None]], axis=1), "ship")
    beta_first = jnp.sqrt(early[:, weeks] / shipments_all + EPS)
    by_beta = (1.0 / beta_first)[:, None]
    p_supplier = ratio * supplier_scale[None, :] * supplier_part * by_beta
    p_week = ratio * week_scale[None, :] * early[:, :weeks] * by_beta
    p_lane = entry * by_beta
    own_square = jnp.sum(p_supplier * p_supplier, axis=1) + entry_square[:, 0] * by_beta[:, 0] * by_beta[:, 0]
    week_square = jnp.sum(p_week * p_week, axis=1)
    effect_square = sum_over(own_square, "ship")
    alpha = jnp.sqrt((effect_square + week_square) / effects_all + EPS)
    by_alpha = (1.0 / alpha)[:, None]
    v_supplier = p_supplier * by_alpha
    v_lane = p_lane * by_alpha
    v_week = p_week * by_alpha
    forward = product(v_supplier * supplier_scale[None, :], supplier_hot.T)
    forward = forward + product(v_week * week_scale[None, :], week_hot.T)
    base = row_weight[None, :] * forward - (alpha[:, None] * by_beta) * rhs

    quarter = lane_own * columns // LANES_WIDE
    slot = (owner ^ me_ship) if by_step else owner
    index = slot * quarter + lane_within % quarter
    lane_part = (lane_within // quarter).reshape(square)
    residual, residual_sum = forward_lanes(
        index, lane_part, row_weight.reshape(square), by_beta * by_alpha, base, tables
    )
    residual_square = sum_over(residual_sum[:, 0], "ship")
    beta_next = jnp.sqrt(residual_square / shipments_all + EPS)
    u_next = residual / beta_next[:, None]
    step_size = alpha * beta_first / (alpha * alpha + beta_next * beta_next)
    x_supplier = step_size[:, None] * v_supplier
    x_lane = step_size[:, None] * v_lane
    effects = jnp.concatenate([jnp.sum(x_supplier * x_supplier, axis=0), jnp.sum(x_lane * x_lane, axis=0)])
    effects = effects + sum(swap(effects, "boot", step) for step in range(1, n_boot))
    spread = jnp.sqrt(effects / (columns * n_boot) + EPS)
    return (v_supplier, v_lane, v_week, u_next, step_size, spread[:supplier_own], spread[supplier_own:])


def solution(mesh):
    return jax.shard_map(
        on_device,
        mesh=mesh,
        in_specs=(
            P("ship"),
            P("ship"),
            P("ship"),
            P("ship", None),
            P("ship"),
            P("ship"),
            P("ship", None),
            P("boot", "ship"),
            P("ship"),
            P("ship"),
            P(),
        ),
        out_specs=(
            P("boot", "ship"),
            P("boot", "ship"),
            P("boot", None),
            P("boot", "ship"),
            P("boot"),
            P("ship"),
            P("ship"),
        ),
        check_vma=False,
    )
```

```python
import functools

import jax
import jax.numpy as jnp
from jax import lax
from jax.experimental import pallas as pl
from jax.experimental.pallas import tpu as pltpu
from jax.sharding import PartitionSpec as P

EPS = 1e-06
BLOCK = 256
FIRSTS = 256
SLOTS = 7
LANES_WIDE = 128
VMEM = pl.BlockSpec(memory_space=pltpu.VMEM)
SMEM = pl.BlockSpec(memory_space=pltpu.SMEM)
ANY = pl.BlockSpec(memory_space=pl.ANY)
PARAMS = pltpu.CompilerParams(vmem_limit_bytes=40 << 20)


SMALL = pltpu.CompilerParams(vmem_limit_bytes=8 << 20)
WHOLE = pltpu.CompilerParams(vmem_limit_bytes=60 << 20)


def takes(microseconds):
    return pl.CostEstimate(flops=0, bytes_accessed=int(microseconds * 3.6e6), transcendentals=0)


def split(value):
    high = value.astype(jnp.bfloat16)
    low = (value - high.astype(jnp.float32)).astype(jnp.bfloat16)
    return high, low


def fetch(sources, held, arrived):
    copies = [pltpu.make_async_copy(source, here, arrived.at[at]) for at, (source, here) in enumerate(zip(sources, held))]
    for copy in copies:
        copy.start()
    for copy in copies:
        copy.wait()
    return held


def held_for(sources):
    return [pltpu.VMEM(one.shape, one.dtype) for one in sources] + [pltpu.SemaphoreType.DMA((len(sources),))]


def swap(value, axis, step):
    size = lax.axis_size(axis)
    return lax.ppermute(value, axis, [(i, i ^ step) for i in range(size)])


def turned(place, size):
    bits = size.bit_length() - 1
    return sum(((place >> bit) & 1) << (bits - 1 - bit) for bit in range(bits))


def sum_over(value, axis, step=1):
    while step < lax.axis_size(axis):
        value = value + swap(value, axis, step)
        step *= 2
    return value


def lane_blocks_kernel(low_n, rows, where, meta, planes, acc, acc_fit):
    blocks = rows * 128 // BLOCK
    offset = where[0]
    shift = low_n.bit_length() - 1
    acc[...] = jnp.zeros_like(acc)
    acc_fit[...] = jnp.zeros_like(acc_fit)
    high_at = lax.broadcasted_iota(jnp.int32, (8, BLOCK), 0)
    place = lax.broadcasted_iota(jnp.int32, (8, BLOCK), 1)
    low_at = lax.broadcasted_iota(jnp.int32, (low_n, BLOCK), 0)

    def two_rows(start):
        pair = [planes[pl.ds(start + u, 1), :] for u in range(BLOCK // 128)]
        return jnp.concatenate(pair, axis=1)

    def prepare(block):
        row = block * (BLOCK // 128)
        local = two_rows(row).astype(jnp.int32) - offset
        high, low = local >> shift, local & (low_n - 1)
        match = jnp.broadcast_to(high, (8, BLOCK)) == high_at
        fit = jnp.where(match, jnp.broadcast_to(two_rows(rows + row), (8, BLOCK)), 0.0)
        res = jnp.where(match, jnp.broadcast_to(two_rows(2 * rows + row), (8, BLOCK)), 0.0)
        hot = jnp.where(jnp.broadcast_to(low, (low_n, BLOCK)) == low_at, 1.0, 0.0).astype(jnp.bfloat16)
        return fit, res, hot

    def group(first, block, fit, res, hot):
        at = place + block * BLOCK
        parts = []
        for u in range(SLOTS):
            inside = (at >= meta[first + u]) & (at < meta[first + u + 1])
            parts.append(jnp.where(inside, res, 0.0))
        left = jnp.concatenate(parts + [fit], axis=0)
        both = lax.dot_general(
            jnp.concatenate(split(left), axis=0),
            hot,
            (((1,), (1,)), ((), ())),
            preferred_element_type=jnp.float32,
        )
        return both[: 8 * SLOTS + 8] + both[8 * SLOTS + 8 :]

    def add(first, sums):
        at = pl.ds(pl.multiple_of(first * 8, 8), 8 * SLOTS)
        for u in range(low_n // 128):
            acc[u, at, :] = acc[u, at, :] + sums[: 8 * SLOTS, u * 128 : (u + 1) * 128]

    unroll = 4

    @pl.loop(0, blocks // unroll)
    def _(step):
        ready = [prepare(step * unroll + u) for u in range(unroll)]
        firsts = [meta[FIRSTS + step * unroll + u] for u in range(unroll)]
        sums = [group(firsts[u], step * unroll + u, *ready[u]) for u in range(unroll)]
        for u in range(unroll):
            add(firsts[u], sums[u])
        acc_fit[...] = acc_fit[...] + sum(one[8 * SLOTS :] for one in sums)
        for u in range(unroll):
            block = step * unroll + u
            more = (meta[FIRSTS + block + 1] - firsts[u]) // SLOTS

            @pl.loop(0, more)
            def _(turn_at):
                first = firsts[u] + (turn_at + 1) * SLOTS
                fit, res, hot = prepare(block)
                add(first, group(first, block, fit, res, hot))


def lane_blocks(where, meta, planes, rows, suppliers, own):
    low_n = max(own // 8, 128)
    return pl.pallas_call(
        functools.partial(lane_blocks_kernel, low_n, rows),
        out_shape=[
            jax.ShapeDtypeStruct((low_n // 128, (suppliers + SLOTS + 1) * 8, 128), jnp.float32),
            jax.ShapeDtypeStruct((8, low_n), jnp.float32),
        ],
        in_specs=[SMEM, SMEM, VMEM],
        out_specs=[VMEM] * 2,
        compiler_params=PARAMS,
        cost_estimate=takes(8),
        name="lane_blocks",
    )(where, meta, planes)


def lane_parts_kernel(turn_n, suppliers, share, where, *refs):
    inputs, outs, signs = refs[:-4], refs[-4:-1], refs[-1]
    accs, fits, got = inputs[:share], inputs[share : 2 * share], inputs[2 * share :]
    columns, own = outs[0].shape
    low_n = fits[0].shape[1]
    at = 0
    for piece in got:
        signs[at : at + piece.shape[0], :] = (2.0 * piece[...] - 1.0).astype(jnp.bfloat16)
        at += piece.shape[0]
    turn = where[1]
    total_fit = fits[0][...]
    for fit in fits[1:]:
        total_fit = total_fit + fit[...]
    height = share * columns
    groups = []
    for part in range(turn_n):
        here = pl.multiple_of((turn ^ turned(part, turn_n)) * height, height)
        groups.append(signs[pl.ds(here, height), :])
    lefts = []
    for step in range(share):
        left = jnp.concatenate([group[step * columns : (step + 1) * columns] for group in groups], axis=0)
        lefts.append(jnp.concatenate([left, left], axis=1))
    for high in range(-(-own // low_n)):
        total = jnp.broadcast_to(total_fit[high : high + 1, :], (turn_n * columns, low_n))
        for step in range(share):
            rows_at = pl.ds(high, suppliers, stride=8)
            wide = jnp.concatenate([accs[step][u, rows_at, :] for u in range(low_n // 128)], axis=1)
            right = jnp.concatenate(split(wide), axis=0)
            total = total + jnp.dot(lefts[step], right, preferred_element_type=jnp.float32)
        for part in range(turn_n):
            if part % 2:
                target, line = 2, (part // 2) * columns
            else:
                target, line = min(part // 2, 1), max(part // 2 - 1, 0) * columns
            value = total[part * columns : (part + 1) * columns]
            outs[target][line : line + columns, high * low_n : (high + 1) * low_n] = value


def lane_parts(where, blocks, got, columns, own, suppliers, turn_n):
    share = len(blocks)
    heights = [n * columns for n in (1, turn_n // 2 - 1, turn_n // 2)]
    return pl.pallas_call(
        functools.partial(lane_parts_kernel, turn_n, suppliers, share),
        out_shape=[jax.ShapeDtypeStruct((height, own), jnp.float32) for height in heights],
        in_specs=[SMEM] + [VMEM] * (2 * share + len(got)),
        out_specs=[VMEM] * 3,
        scratch_shapes=[pltpu.VMEM((turn_n * share * columns, suppliers), jnp.bfloat16)],
        compiler_params=PARAMS,
        cost_estimate=takes(1),
        name="lane_parts",
    )(where, *[acc for acc, _ in blocks], *[fit for _, fit in blocks], *got)


def table_kernel(ratio, scale, own, *refs):
    parts, entries, table = refs[:-2], refs[-2], refs[-1]
    total = parts[0][...]
    for part in parts[1:]:
        total = total + part[...]
    by = jnp.broadcast_to(scale[...], total.shape)
    entry = ratio * by * total
    entries[...] = entry
    columns = total.shape[0]
    square = jnp.sum(entry * entry, axis=1, keepdims=True) + own[...]
    wide = jnp.broadcast_to(square, (columns, 128))
    scaled = by * entry
    quarter = table.shape[0] - 8
    count = total.shape[1] // quarter
    stacked = jnp.concatenate([scaled[:, u * quarter : (u + 1) * quarter] for u in range(count)], axis=0)
    table[0:quarter, :] = stacked.T
    table[quarter:, :] = jnp.concatenate([wide] * (128 // columns), axis=0).T[0:8]


def lane_table(ratio, scale, own, parts):
    columns, lanes = parts[0].shape
    quarter = lanes * columns // LANES_WIDE
    return pl.pallas_call(
        functools.partial(table_kernel, ratio),
        out_shape=[
            jax.ShapeDtypeStruct((columns, lanes), jnp.float32),
            jax.ShapeDtypeStruct((quarter + 8, LANES_WIDE), jnp.float32),
        ],
        in_specs=[VMEM] * (2 + len(parts)),
        out_specs=[VMEM] * 2,
        compiler_params=SMALL,
        cost_estimate=takes(1),
        name="lane_table",
    )(scale, own, *parts)


def forward_kernel(effects_all, lines, index, before, by_beta, week_square, lane_part, weight, *refs):
    sources, tables = refs[:2], refs[2:-12]
    out, squares, alpha_out, table, first, second, total, forward, rhs, value_out, landed, moved = refs[-12:]
    columns = total.shape[0]
    groups = weight.shape[0]
    copies, at = [], 0
    for place, piece in enumerate(tables):
        here = table.at[pl.ds(at, piece.shape[0])]
        copies.append(pltpu.make_async_copy(piece, here, landed.at[place]))
        at += piece.shape[0]
    parts = 4
    wide = groups * 128 // parts
    loads = []
    for part in range(parts):
        here = (slice(None), pl.ds(part * wide, wide))
        for place, (source, held) in enumerate(zip(sources, (forward, rhs))):
            loads.append(pltpu.make_async_copy(source.at[here], held.at[here], moved.at[place, part]))
    for copy in [*copies, *loads]:
        copy.start()
    for copy in copies:
        copy.wait()
    effect_square = jnp.zeros((1, 128), jnp.float32)
    for start in range(0, at, lines + 8):
        effect_square = effect_square + table[start + lines : start + lines + 1, :]
    effect_square = jnp.broadcast_to(effect_square, (128, 128)).T[0:columns]
    by = by_beta[...]
    alpha = jnp.sqrt((effect_square[:, 0:1] * by * by + week_square[...]) / effects_all + EPS)
    alpha_out[...] = alpha
    scale = jnp.broadcast_to(by / alpha, (columns, 128))
    share = jnp.broadcast_to(by * alpha, (columns, 128))
    total[...] = jnp.zeros_like(total)

    def gather(group, store):
        for u in range(128):
            store[u : u + 1, :] = table[pl.ds(index[group * 128 + u], 1), :]

    def finish(group, store):
        turned_over = store[...].T
        part = jnp.broadcast_to(lane_part[pl.ds(group, 1), :], (columns, 128))
        picked = turned_over[0:columns]
        for u in range(1, 128 // columns):
            picked = jnp.where(part == u, turned_over[u * columns : (u + 1) * columns], picked)
        at = pl.ds(pl.multiple_of(group * 128, 128), 128)
        line = jnp.broadcast_to(weight[pl.ds(group, 1), :], (columns, 128))
        value = (forward[:, at] + picked * line) * scale - share * rhs[:, at]
        value_out[:, at] = value
        total[...] = total[...] + value * value

    gather(0, first)
    stores = []
    for part in range(parts):
        for copy in loads[2 * part : 2 * part + 2]:
            copy.wait()

        @pl.loop(part * groups // 2 // parts, (part + 1) * groups // 2 // parts)
        def _(step):
            gather(2 * step + 1, second)
            finish(2 * step, first)
            gather(jnp.minimum(2 * step + 2, groups - 1), first)
            finish(2 * step + 1, second)

        here = (slice(None), pl.ds(part * wide, wide))
        stores.append(pltpu.make_async_copy(value_out.at[here], out.at[here], moved.at[2, part]))
        stores[-1].start()
    across = jnp.broadcast_to(jnp.sum(total[...], axis=1, keepdims=True), (columns, 128))
    squares[...] = jnp.concatenate([across] * (128 // columns), axis=0).T[0:8]
    for copy in stores:
        copy.wait()


def forward_lanes(effects_all, lines, index, before, by_beta, week_square, lane_part, weight, forward, rhs, tables):
    columns, rows = rhs.shape
    height = sum(piece.shape[0] for piece in tables)
    return pl.pallas_call(
        functools.partial(forward_kernel, effects_all, lines),
        out_shape=[
            jax.ShapeDtypeStruct((columns, rows), jnp.float32),
            jax.ShapeDtypeStruct((8, 128), jnp.float32),
            jax.ShapeDtypeStruct((columns, 1), jnp.float32),
        ],
        in_specs=[SMEM] + [VMEM] * 5 + [ANY] * (2 + len(tables)),
        out_specs=[ANY] + [VMEM] * 2,
        scratch_shapes=[
            pltpu.VMEM((height, LANES_WIDE), jnp.float32),
            pltpu.VMEM((128, LANES_WIDE), jnp.float32),
            pltpu.VMEM((128, LANES_WIDE), jnp.float32),
            pltpu.VMEM((columns, 128), jnp.float32),
            *[pltpu.VMEM((columns, rows), jnp.float32)] * 3,
            pltpu.SemaphoreType.DMA((len(tables),)),
            pltpu.SemaphoreType.DMA((3, 4)),
        ],
        compiler_params=WHOLE,
        cost_estimate=takes(18),
        name="forward_lanes",
    )(index, before, by_beta, week_square, lane_part, weight, forward, rhs, *tables)


def message_kernel(lane_own, *refs):
    sources, (planes, bounds, firsts), held, arrived = refs[:7], refs[7:10], refs[10:17], refs[17]
    fitted, resid, weight, block, within, runs, signs = fetch(sources, held, arrived)
    rows = fitted.shape[0]
    planes[0:rows, :] = (block[...] * lane_own + within[...]).astype(jnp.float32)
    planes[rows : 2 * rows, :] = weight[...] * fitted[...]
    planes[2 * rows : 3 * rows, :] = weight[...] * resid[...]
    suppliers = runs.shape[1]
    across = jnp.broadcast_to(runs[...].astype(jnp.float32), (suppliers, suppliers))
    down = across.T
    at_row = lax.broadcasted_iota(jnp.int32, (suppliers, suppliers), 0)
    at_lane = lax.broadcasted_iota(jnp.int32, (suppliers, suppliers), 1)
    end_column = jnp.sum(jnp.where(at_lane <= at_row, across, 0.0), axis=1, keepdims=True)
    start_column = jnp.sum(jnp.where(at_lane < at_row, across, 0.0), axis=1, keepdims=True)
    start_row = jnp.sum(jnp.where(at_row < at_lane, down, 0.0), axis=0, keepdims=True)
    whole = (at_lane * BLOCK).astype(jnp.float32)
    first_row = jnp.sum(jnp.where(end_column <= whole, 1.0, 0.0), axis=0, keepdims=True)
    full = jnp.full((1, suppliers), rows * 128.0, jnp.float32)
    planes[3 * rows + 8 :, :] = signs[...].astype(jnp.float32)
    planes[3 * rows : 3 * rows + 8, :] = jnp.concatenate(
        [start_row, full, first_row, jnp.zeros((5, suppliers), jnp.float32)], axis=0
    )
    firsts[...] = first_row.astype(jnp.int32)
    columns = [start_column, end_column, jnp.zeros((suppliers, 6), jnp.float32)]
    bounds[0:suppliers, :] = jnp.concatenate(columns, axis=1).astype(jnp.int32)
    bounds[suppliers:, :] = jnp.full((16, 8), rows * 128, jnp.int32)


def message(lane_own, *sources):
    fitted, runs, signs = sources[0], sources[5], sources[6]
    rows = fitted.shape[0]
    suppliers = runs.shape[1]
    return pl.pallas_call(
        functools.partial(message_kernel, lane_own),
        out_shape=[
            jax.ShapeDtypeStruct((3 * rows + 8 + signs.shape[0], 128), jnp.float32),
            jax.ShapeDtypeStruct((suppliers + 16, 8), jnp.int32),
            jax.ShapeDtypeStruct((1, suppliers), jnp.int32),
        ],
        in_specs=[ANY] * 7,
        out_specs=[VMEM] * 3,
        scratch_shapes=held_for(sources),
        compiler_params=WHOLE,
        cost_estimate=takes(2),
        name="message",
    )(*sources)


def row_of(ref, start):
    pair = [ref[pl.ds(start + u, 1), :] for u in range(BLOCK // 128)]
    return jnp.concatenate(pair, axis=1)


def hot_supplier(block, bounds):
    suppliers = bounds.shape[0] - 16
    place = lax.broadcasted_iota(jnp.int32, (suppliers, BLOCK), 1) + block * BLOCK
    inside = (place >= bounds[0:suppliers, 0:1]) & (place < bounds[0:suppliers, 1:2])
    return jnp.where(inside, 1.0, 0.0).astype(jnp.bfloat16)


def hot_week(block, week, weeks):
    at = lax.broadcasted_iota(jnp.int32, (weeks, BLOCK), 0)
    same = jnp.broadcast_to(row_of(week, block * (BLOCK // 128)), (weeks, BLOCK)) == at
    return jnp.where(same, 1.0, 0.0).astype(jnp.bfloat16)


def own_sums_kernel(weeks, firsts, *refs):
    supplier, stats, by_week, fit_week, by_sign = refs[6], refs[7], *refs[-3:]
    fitted, resid, weight, week, bounds, signs = fetch(refs[:6], refs[8:14], refs[14])
    columns, suppliers = signs.shape
    blocks = fitted.shape[0] * 128 // BLOCK
    by_week[...] = jnp.zeros_like(by_week)
    fit_week[...] = jnp.zeros_like(fit_week)
    by_sign[...] = jnp.zeros_like(by_sign)
    shape = (8, BLOCK)
    place = lax.broadcasted_iota(jnp.int32, shape, 1)
    line = lax.broadcasted_iota(jnp.int32, shape, 0)

    def prepare(block):
        row = block * (BLOCK // 128)
        fit, res, by = [jnp.broadcast_to(row_of(one, row), shape) for one in (fitted, resid, weight)]
        more, less = fit + res, fit - res
        both = jnp.where(line == 0, more * more, jnp.where(line == 1, less * less, 0.0))
        both = jnp.where(line == 2, by * more, jnp.where(line == 3, by * less, both))
        return jnp.where(line == 0, by * fit, 0.0), by * res, both, hot_week(block, week, weeks)

    def group(first, block, fit, res, both, hot):
        at = place + block * BLOCK
        here = bounds[pl.ds(first, 8), :]
        inside = (at >= here[:, 0:1]) & (at < here[:, 1:2])
        left = jnp.concatenate([jnp.where(inside, res, 0.0), fit], axis=0)
        left = jnp.concatenate(split(left), axis=0)
        sums = lax.dot_general(left, hot, (((1,), (1,)), ((), ())), preferred_element_type=jnp.float32)
        mask = jnp.where(jnp.concatenate([inside, inside], axis=0), 1.0, 0.0).astype(jnp.bfloat16)
        pair = jnp.concatenate(split(both), axis=0)
        signed = lax.dot_general(mask, pair, (((1,), (1,)), ((), ())), preferred_element_type=jnp.float32)
        return sums[:16] + sums[16:], signed[:8]

    def add(first, got):
        at = pl.ds(first, 8)
        for u in range(by_week.shape[0]):
            part = got[0][:8, u * 128 : (u + 1) * 128]
            wide = slice(0, part.shape[1])
            by_week[u, at, wide] = by_week[u, at, wide] + part
        by_sign[at, 0:16] = by_sign[at, 0:16] + got[1]

    unroll = 4

    @pl.loop(0, blocks // unroll)
    def _(step):
        ready = [prepare(step * unroll + u) for u in range(unroll)]
        begin = [firsts[0, step * unroll + u] for u in range(unroll)]
        got = [group(begin[u], step * unroll + u, *ready[u]) for u in range(unroll)]
        for u in range(unroll):
            add(begin[u], got[u])
        fit_week[:, 0:weeks] = fit_week[:, 0:weeks] + sum(one[0][8:] for one in got)
        for u in range(unroll):
            block = step * unroll + u

            @pl.loop(0, (firsts[0, block + 1] - begin[u]) // 8)
            def _(turn_at):
                first = begin[u] + (turn_at + 1) * 8
                fit, res, both, hot = prepare(block)
                add(first, group(first, block, fit, res, both, hot))

    positive = signs[...] == 1
    sign = (2 * signs[...] - 1).astype(jnp.float32).astype(jnp.bfloat16)
    left = jnp.concatenate([sign, sign], axis=1)
    four = by_sign[0:suppliers, :].T
    four = four[0:8] + four[8:16]
    rows = [jnp.broadcast_to(four[u : u + 1, :], positive.shape) for u in range(4)]
    supplier[...] = jnp.where(positive, rows[2], rows[3])
    square = jnp.broadcast_to(jnp.sum(jnp.where(positive, rows[0], rows[1]), axis=1, keepdims=True), (columns, 128))
    last = lax.broadcasted_iota(jnp.int32, (columns, 128), 1) == 127
    for u in range(by_week.shape[0]):
        right = jnp.concatenate(split(by_week[u, 0:suppliers, :]), axis=0)
        part = fit_week[0:1, u * 128 : u * 128 + 128]
        part = jnp.dot(left, right, preferred_element_type=jnp.float32) + jnp.broadcast_to(part, (columns, 128))
        if u == by_week.shape[0] - 1:
            part = jnp.where(last, square, part)
        stats[u * columns : (u + 1) * columns, :] = part


def own_sums(firsts, weeks, *sources):
    columns, suppliers = sources[5].shape
    return pl.pallas_call(
        functools.partial(own_sums_kernel, weeks),
        out_shape=[
            jax.ShapeDtypeStruct((columns, suppliers), jnp.float32),
            jax.ShapeDtypeStruct((-(-weeks // 128) * columns, 128), jnp.float32),
        ],
        in_specs=[SMEM] + [ANY] * 6,
        out_specs=[VMEM] * 2,
        scratch_shapes=held_for(sources)
        + [
            pltpu.VMEM((-(-weeks // 128), suppliers + 16, 128), jnp.float32),
            pltpu.VMEM((8, -(-weeks // 128) * 128), jnp.float32),
            pltpu.VMEM((suppliers + 16, 128), jnp.float32),
        ],
        compiler_params=WHOLE,
        cost_estimate=takes(7),
        name="own_sums",
    )(firsts, *sources)


def base_kernel(*refs):
    forward, rhs_out, token = refs[8:11]
    fitted, resid, weight, week, bounds, signs, effects = fetch(refs[:7], refs[11:18], refs[18])
    columns, suppliers = signs.shape
    weeks = effects.shape[1] - suppliers
    sign = (2 * signs[...] - 1).astype(jnp.float32).astype(jnp.bfloat16)
    by_effect = jnp.concatenate(split(effects[...]), axis=0)
    blocks = fitted.shape[0] * 128 // BLOCK

    def one(block):
        row = block * (BLOCK // 128)
        by_supplier = hot_supplier(block, bounds)
        spread = jnp.dot(sign, by_supplier, preferred_element_type=jnp.float32)
        shape = (columns, BLOCK)
        at = pl.ds(pl.multiple_of(block * BLOCK, BLOCK), BLOCK)
        rhs = jnp.broadcast_to(row_of(fitted, row), shape) + spread * jnp.broadcast_to(row_of(resid, row), shape)
        rhs_out[:, at] = rhs
        hot = jnp.concatenate([by_supplier, hot_week(block, week, weeks)], axis=0)
        both = jnp.dot(by_effect, hot, preferred_element_type=jnp.float32)
        forward[:, at] = jnp.broadcast_to(row_of(weight, row), shape) * (both[:columns] + both[columns:])

    unroll = 4

    @pl.loop(0, blocks // unroll)
    def _(step):
        for u in range(unroll):
            one(step * unroll + u)

    token[...] = jnp.zeros_like(token)


def forward_base(sources, before):
    shape = jax.ShapeDtypeStruct((sources[5].shape[0], sources[0].size), jnp.float32)
    return pl.pallas_call(
        base_kernel,
        out_shape=[shape, shape, jax.ShapeDtypeStruct((8, 128), jnp.float32)],
        in_specs=[ANY] * 8,
        out_specs=[VMEM] * 3,
        scratch_shapes=held_for(sources),
        compiler_params=PARAMS,
        cost_estimate=takes(8),
        name="forward_base",
    )(*sources, before)


def near_tables(table, n_ship):
    if n_ship > 16:
        return [lax.all_gather(table, "ship", axis=0, tiled=True)]
    steps = [*range(1, n_ship // 2), *range(n_ship // 2, n_ship, 2)]
    return [table] + [swap(table, "ship", step) for step in steps]


def all_tables(near, n_ship):
    if n_ship > 16:
        return near
    tables = near[: n_ship // 2]
    for table in near[n_ship // 2 :]:
        tables += [table, swap(table, "ship", 1)]
    return tables


def effect_sums_kernel(count, residual, alpha, beta_first, supplier, entry, sums, step_out, inverse):
    columns = alpha.shape[0]
    square = jnp.broadcast_to(residual[0:1, :], (128, 128)).T[0:columns, 0:1]
    beta_next = jnp.sqrt(square / count + EPS)
    step = alpha[...] * beta_first[...] / (alpha[...] * alpha[...] + beta_next * beta_next)
    step_out[...] = step
    inverse[...] = 1.0 / beta_next
    scale = step / (alpha[...] * beta_first[...])
    rows = []
    for line in (supplier[...] * scale, entry[...] * scale):
        total = jnp.sum(line * line, axis=0, keepdims=True)
        rows += [total[:, at : at + 128] for at in range(0, line.shape[1], 128)]
    rows.append(jnp.zeros((sums.shape[0] - len(rows), 128), jnp.float32))
    sums[...] = jnp.concatenate(rows, axis=0)


def effect_sums(count, residual, alpha, beta_first, supplier, entry):
    lines = 1 + entry.shape[1] // 128
    column = jax.ShapeDtypeStruct(alpha.shape, jnp.float32)
    return pl.pallas_call(
        functools.partial(effect_sums_kernel, count),
        out_shape=[jax.ShapeDtypeStruct((lines // 8 * 8 + 8, 128), jnp.float32), column, column],
        in_specs=[VMEM] * 5,
        out_specs=[VMEM] * 3,
        compiler_params=SMALL,
        cost_estimate=takes(1),
        name="effect_sums",
    )(residual, alpha, beta_first, supplier, entry)


def spread_kernel(count, *refs):
    parts, supplier, lane = refs[:-2], refs[-2], refs[-1]
    total = parts[0][...]
    for part in parts[1:]:
        total = total + part[...]
    total = jnp.sqrt(total / count + EPS)
    supplier[...] = total[0:1]
    lane[...] = total[1 : 1 + lane.shape[0]]


def spreads(count, lines, parts):
    return pl.pallas_call(
        functools.partial(spread_kernel, count),
        out_shape=[jax.ShapeDtypeStruct((1, 128), jnp.float32), jax.ShapeDtypeStruct((lines, 128), jnp.float32)],
        in_specs=[VMEM] * len(parts),
        out_specs=[VMEM] * 2,
        compiler_params=SMALL,
        cost_estimate=takes(1),
        name="spreads",
    )(*parts)


def on_device(
    fitted,
    resid,
    row_weight,
    lane_block,
    lane_within,
    week_id,
    supplier_runs,
    signs,
    supplier_scale,
    lane_scale,
    week_scale,
):
    rows = fitted.shape[0]
    columns = signs.shape[0]
    n_ship = lax.axis_size("ship")
    n_boot = lax.axis_size("boot")
    me_ship = lax.axis_index("ship")
    me_boot = lax.axis_index("boot")
    lane_own = lane_scale.shape[0]
    weeks = week_scale.shape[0]
    supplier_own = supplier_scale.shape[0]
    shipments_all = rows * n_ship
    effects_all = supplier_own * n_ship + lane_own * n_ship + weeks
    ratio = effects_all / shipments_all
    share = n_ship // n_boot

    owner = lane_block[:, 0]
    square = (rows // 128, 128)
    fitted, resid, row_weight, week_id = [one.reshape(square) for one in (fitted, resid, row_weight, week_id)]

    planes, bounds, firsts = message(
        lane_own, fitted, resid, row_weight, owner.reshape(square), lane_within.reshape(square), supplier_runs, signs
    )
    got = []
    for turn in range(share):
        pairs = []
        for source in range(n_ship):
            target = (source // n_boot - turn) % share * n_boot
            for b in range(n_boot):
                pairs.append((source * n_boot + b, (target + turned(b, n_boot)) * n_boot + source % n_boot))
        got.append(lax.ppermute(planes, ("ship", "boot"), pairs))

    weeks_up = -(-weeks // 16) * 16
    held = (fitted, resid, row_weight, week_id, bounds, signs)
    supplier_part, early = own_sums(firsts, weeks_up, *held)
    got, early = lax.optimization_barrier((got, early))
    p_supplier = ratio * supplier_scale[None, :] * supplier_part
    supplier_square = jnp.sum(p_supplier * p_supplier, axis=1, keepdims=True)

    me_turn = sum(jnp.where(me_boot == b, turned(b, n_boot), 0) for b in range(n_boot))
    where = jnp.stack([me_ship * lane_own, (me_ship % n_boot) ^ me_turn]).astype(jnp.int32)
    fixed = 3 * square[0] + 8
    others = [one[fixed:] for one in got]
    blocks, step = [], 1
    for at, one in enumerate(got):
        meta = one[fixed - 8 : fixed].reshape(-1).astype(jnp.int32)
        blocks.append(lane_blocks(where, meta, one, square[0], supplier_own, lane_own))
        if step < n_boot:
            lines = step * share * columns
            back = swap(jnp.concatenate([*others, early], axis=0), "ship", step)
            others, early, step = [*others, back[:lines]], early + back[lines:], 2 * step
            if at + 1 < share:
                got[at + 1], early = lax.optimization_barrier((got[at + 1], early))
    early = sum_over(early, "ship", step)
    sums = lane_parts(where, blocks, others, columns, lane_own, supplier_own, n_boot)
    kept, later, sent = sums
    back = swap(sent, "boot", 1)
    pieces = [kept, back[:columns]]
    later = later + back[columns:]
    for step in range(1, n_boot // 2):
        pieces.append(swap(later[(step - 1) * columns : step * columns], "boot", 2 * step))
    entry, table = lane_table(ratio, lane_scale[None, :], supplier_square, pieces)
    near = near_tables(table, n_ship)

    beta_first = jnp.sqrt(early[-columns:, 127] / shipments_all + EPS)
    week_part = jnp.concatenate([early[at : at + columns] for at in range(0, early.shape[0], columns)], axis=1)
    by_beta = (1.0 / beta_first)[:, None]
    p_week = ratio * week_scale[None, :] * week_part[:, :weeks]
    week_square = jnp.sum(p_week * p_week, axis=1, keepdims=True) * by_beta * by_beta
    effects = jnp.concatenate(
        [
            p_supplier * supplier_scale[None, :],
            p_week * week_scale[None, :],
            jnp.zeros((columns, weeks_up - weeks), jnp.float32),
        ],
        axis=1,
    )

    forward, rhs, token = forward_base((*held, effects), near[min(1, len(near) - 1)][:8])
    near[n_ship // 2 :], token = lax.optimization_barrier((near[n_ship // 2 :], token))
    tables = all_tables(near, n_ship)

    quarter = lane_own * columns // LANES_WIDE
    slot = owner if n_ship > 16 else owner ^ me_ship
    index = slot * (quarter + 8) + lane_within % quarter
    lane_part = (lane_within // quarter).reshape(square)
    residual, residual_sum, alpha = forward_lanes(
        effects_all, quarter, index, token, by_beta, week_square, lane_part, row_weight, forward, rhs, tables
    )
    by_both = by_beta / alpha
    v_supplier = p_supplier * by_both
    v_lane = entry * by_both
    v_week = p_week * by_both
    residual_sum = sum_over(residual_sum, "ship")
    effects, step_size, inverse = effect_sums(shipments_all, residual_sum, alpha, beta_first[:, None], p_supplier, entry)
    effects = [effects] + [swap(effects, "boot", step) for step in range(1, n_boot)]
    u_next = residual * inverse
    spread_supplier, spread_lane = spreads(columns * n_boot, lane_own // 128, effects)
    spread_supplier, spread_lane = spread_supplier.reshape(-1), spread_lane.reshape(-1)
    return (v_supplier, v_lane, v_week, u_next, step_size[:, 0], spread_supplier, spread_lane)


def solution(mesh):
    return jax.shard_map(
        on_device,
        mesh=mesh,
        in_specs=(
            P("ship"),
            P("ship"),
            P("ship"),
            P("ship", None),
            P("ship"),
            P("ship"),
            P("ship", None),
            P("boot", "ship"),
            P("ship"),
            P("ship"),
            P(),
        ),
        out_specs=(
            P("boot", "ship"),
            P("boot", "ship"),
            P("boot", None),
            P("boot", "ship"),
            P("boot"),
            P("ship"),
            P("ship"),
        ),
        check_vma=False,
    )
```

```python
import functools

import jax
import jax.numpy as jnp
from jax import lax
from jax.experimental import pallas as pl
from jax.experimental.pallas import tpu as pltpu
from jax.sharding import PartitionSpec as P

EPS = 1e-06
BLOCK = 256
FIRSTS = 256
SLOTS = 7
LANES_WIDE = 128
VMEM = pl.BlockSpec(memory_space=pltpu.VMEM)
SMEM = pl.BlockSpec(memory_space=pltpu.SMEM)
HBM = pl.BlockSpec(memory_space=pltpu.HBM)
PARAMS = pltpu.CompilerParams(vmem_limit_bytes=40 << 20)


WHOLE = pltpu.CompilerParams(vmem_limit_bytes=60 << 20)
SMALL = pltpu.CompilerParams(vmem_limit_bytes=8 << 20)


def takes(microseconds):
    return pl.CostEstimate(flops=0, bytes_accessed=int(microseconds * 3.6e6), transcendentals=0)


def split(value):
    high = value.astype(jnp.bfloat16)
    low = (value - high.astype(jnp.float32)).astype(jnp.bfloat16)
    return high, low


def fetch(sources, held, arrived):
    copies = [pltpu.make_async_copy(source, here, arrived.at[at]) for at, (source, here) in enumerate(zip(sources, held))]
    for copy in copies:
        copy.start()
    for copy in copies:
        copy.wait()
    return held


def held_for(sources):
    return [pltpu.VMEM(one.shape, one.dtype) for one in sources] + [pltpu.SemaphoreType.DMA((len(sources),))]


def swap(value, axis, step):
    size = lax.axis_size(axis)
    return lax.ppermute(value, axis, [(i, i ^ step) for i in range(size)])


def turned(place, size):
    bits = size.bit_length() - 1
    return sum(((place >> bit) & 1) << (bits - 1 - bit) for bit in range(bits))


def sum_over(value, axis, step=1):
    while step < lax.axis_size(axis):
        value = value + swap(value, axis, step)
        step *= 2
    return value


def lane_blocks_kernel(low_n, rows, where, meta, planes, acc, acc_fit):
    blocks = rows * 128 // BLOCK
    offset = where[0]
    shift = low_n.bit_length() - 1
    acc[...] = jnp.zeros_like(acc)
    acc_fit[...] = jnp.zeros_like(acc_fit)
    high_at = lax.broadcasted_iota(jnp.int32, (8, BLOCK), 0)
    place = lax.broadcasted_iota(jnp.int32, (8, BLOCK), 1)
    low_at = lax.broadcasted_iota(jnp.int32, (low_n, BLOCK), 0)

    def two_rows(start):
        pair = [planes[pl.ds(start + u, 1), :] for u in range(BLOCK // 128)]
        return jnp.concatenate(pair, axis=1)

    def prepare(block):
        row = block * (BLOCK // 128)
        local = two_rows(row).astype(jnp.int32) - offset
        high, low = local >> shift, local & (low_n - 1)
        match = jnp.broadcast_to(high, (8, BLOCK)) == high_at
        fit = jnp.where(match, jnp.broadcast_to(two_rows(rows + row), (8, BLOCK)), 0.0)
        res = jnp.where(match, jnp.broadcast_to(two_rows(2 * rows + row), (8, BLOCK)), 0.0)
        hot = jnp.where(jnp.broadcast_to(low, (low_n, BLOCK)) == low_at, 1.0, 0.0).astype(jnp.bfloat16)
        return fit, res, hot

    def group(first, block, fit, res, hot):
        at = place + block * BLOCK
        parts = []
        for u in range(SLOTS):
            inside = (at >= meta[first + u]) & (at < meta[first + u + 1])
            parts.append(jnp.where(inside, res, 0.0))
        left = jnp.concatenate(parts + [fit], axis=0)
        both = lax.dot_general(
            jnp.concatenate(split(left), axis=0),
            hot,
            (((1,), (1,)), ((), ())),
            preferred_element_type=jnp.float32,
        )
        return both[: 8 * SLOTS + 8] + both[8 * SLOTS + 8 :]

    def add(first, sums):
        at = pl.ds(pl.multiple_of(first * 8, 8), 8 * SLOTS)
        for u in range(low_n // 128):
            acc[u, at, :] = acc[u, at, :] + sums[: 8 * SLOTS, u * 128 : (u + 1) * 128]

    unroll = 8

    @pl.loop(0, blocks // unroll)
    def _(step):
        ready = [prepare(step * unroll + u) for u in range(unroll)]
        firsts = [meta[FIRSTS + step * unroll + u] for u in range(unroll)]
        sums = [group(firsts[u], step * unroll + u, *ready[u]) for u in range(unroll)]
        for u in range(unroll):
            add(firsts[u], sums[u])
        acc_fit[...] = acc_fit[...] + sum(one[8 * SLOTS :] for one in sums)
        ends = firsts[1:] + [meta[FIRSTS + (step + 1) * unroll]]
        more = sum((end - first) // SLOTS for first, end in zip(firsts, ends))

        @pl.when(more > 0)
        def _():
            @pl.loop(0, unroll)
            def _(u):
                block = step * unroll + u
                begin = meta[FIRSTS + block]

                @pl.loop(0, (meta[FIRSTS + block + 1] - begin) // SLOTS)
                def _(turn_at):
                    first = begin + (turn_at + 1) * SLOTS
                    fit, res, hot = prepare(block)
                    add(first, group(first, block, fit, res, hot))


def lane_blocks(where, meta, planes, rows, suppliers, own):
    low_n = max(own // 8, 128)
    return pl.pallas_call(
        functools.partial(lane_blocks_kernel, low_n, rows),
        out_shape=[
            jax.ShapeDtypeStruct((low_n // 128, (suppliers + SLOTS + 1) * 8, 128), jnp.float32),
            jax.ShapeDtypeStruct((8, low_n), jnp.float32),
        ],
        in_specs=[SMEM, SMEM, VMEM],
        out_specs=[VMEM] * 2,
        compiler_params=PARAMS,
        cost_estimate=takes(8),
        name="lane_blocks",
    )(where, meta, planes)


def lane_parts_kernel(turn_n, suppliers, share, where, *refs):
    inputs, outs, signs = refs[:-4], refs[-4:-1], refs[-1]
    accs, fits, got = inputs[:share], inputs[share : 2 * share], inputs[2 * share :]
    columns, own = outs[0].shape
    low_n = fits[0].shape[1]
    at = 0
    for piece in got:
        signs[at : at + piece.shape[0], :] = (2.0 * piece[...] - 1.0).astype(jnp.bfloat16)
        at += piece.shape[0]
    turn = where[1]
    total_fit = fits[0][...]
    for fit in fits[1:]:
        total_fit = total_fit + fit[...]
    height = share * columns
    groups = []
    for part in range(turn_n):
        here = pl.multiple_of((turn ^ turned(part, turn_n)) * height, height)
        groups.append(signs[pl.ds(here, height), :])
    lefts = []
    for step in range(share):
        left = jnp.concatenate([group[step * columns : (step + 1) * columns] for group in groups], axis=0)
        lefts.append(jnp.concatenate([left, left], axis=1))
    for high in range(-(-own // low_n)):
        total = jnp.broadcast_to(total_fit[high : high + 1, :], (turn_n * columns, low_n))
        for step in range(share):
            rows_at = pl.ds(high, suppliers, stride=8)
            wide = jnp.concatenate([accs[step][u, rows_at, :] for u in range(low_n // 128)], axis=1)
            right = jnp.concatenate(split(wide), axis=0)
            total = total + jnp.dot(lefts[step], right, preferred_element_type=jnp.float32)
        for part in range(turn_n):
            if part % 2:
                target, line = 2, (part // 2) * columns
            else:
                target, line = min(part // 2, 1), max(part // 2 - 1, 0) * columns
            value = total[part * columns : (part + 1) * columns]
            outs[target][line : line + columns, high * low_n : (high + 1) * low_n] = value


def lane_parts(where, blocks, got, columns, own, suppliers, turn_n):
    share = len(blocks)
    heights = [n * columns for n in (1, turn_n // 2 - 1, turn_n // 2)]
    return pl.pallas_call(
        functools.partial(lane_parts_kernel, turn_n, suppliers, share),
        out_shape=[jax.ShapeDtypeStruct((height, own), jnp.float32) for height in heights],
        in_specs=[SMEM] + [VMEM] * (2 * share + len(got)),
        out_specs=[VMEM] * 3,
        scratch_shapes=[pltpu.VMEM((turn_n * share * columns, suppliers), jnp.bfloat16)],
        compiler_params=PARAMS,
        cost_estimate=takes(1),
        name="lane_parts",
    )(where, *[acc for acc, _ in blocks], *[fit for _, fit in blocks], *got)


def table_kernel(ratio, scale, own, *refs):
    parts, entries, table = refs[:-2], refs[-2], refs[-1]
    total = parts[0][...]
    for part in parts[1:]:
        total = total + part[...]
    by = jnp.broadcast_to(scale[...], total.shape)
    entry = ratio * by * total
    entries[...] = entry
    columns = total.shape[0]
    square = jnp.sum(entry * entry, axis=1, keepdims=True) + own[...]
    wide = jnp.broadcast_to(square, (columns, 128))
    scaled = by * entry
    quarter = table.shape[0] - 8
    count = total.shape[1] // quarter
    stacked = jnp.concatenate([scaled[:, u * quarter : (u + 1) * quarter] for u in range(count)], axis=0)
    table[0:quarter, :] = stacked.T
    table[quarter:, :] = jnp.concatenate([wide] * (128 // columns), axis=0).T[0:8]


def lane_table(ratio, scale, own, parts):
    columns, lanes = parts[0].shape
    quarter = lanes * columns // LANES_WIDE
    return pl.pallas_call(
        functools.partial(table_kernel, ratio),
        out_shape=[
            jax.ShapeDtypeStruct((columns, lanes), jnp.float32),
            jax.ShapeDtypeStruct((quarter + 8, LANES_WIDE), jnp.float32),
        ],
        in_specs=[VMEM] * (2 + len(parts)),
        out_specs=[VMEM] * 2,
        compiler_params=SMALL,
        cost_estimate=takes(1),
        name="lane_table",
    )(scale, own, *parts)


def forward_kernel(effects_all, lines, index, before, by_beta, week_square, lane_part, weight, forward, rhs, *refs):
    tables, (out, squares, alpha_out, table, first, second, total, landed) = refs[:-8], refs[-8:]
    columns = out.shape[0]
    copies, at = [], 0
    for place, piece in enumerate(tables):
        here = table.at[pl.ds(at, piece.shape[0])]
        copies.append(pltpu.make_async_copy(piece, here, landed.at[place]))
        at += piece.shape[0]
    for copy in copies:
        copy.start()
    for copy in copies:
        copy.wait()
    effect_square = jnp.zeros((1, 128), jnp.float32)
    for start in range(0, at, lines + 8):
        effect_square = effect_square + table[start + lines : start + lines + 1, :]
    effect_square = jnp.broadcast_to(effect_square, (128, 128)).T[0:columns]
    by = by_beta[...]
    alpha = jnp.sqrt((effect_square[:, 0:1] * by * by + week_square[...]) / effects_all + EPS)
    alpha_out[...] = alpha
    scale = jnp.broadcast_to(by / alpha, (columns, 128))
    share = jnp.broadcast_to(by * alpha, (columns, 128))
    groups = weight.shape[0]
    total[...] = jnp.zeros_like(total)

    def gather(group, store):
        for u in range(128):
            store[u : u + 1, :] = table[pl.ds(index[group * 128 + u], 1), :]

    def finish(group, store):
        turned_over = store[...].T
        part = jnp.broadcast_to(lane_part[pl.ds(group, 1), :], (columns, 128))
        picked = turned_over[0:columns]
        for u in range(1, 128 // columns):
            picked = jnp.where(part == u, turned_over[u * columns : (u + 1) * columns], picked)
        at = pl.ds(pl.multiple_of(group * 128, 128), 128)
        by = jnp.broadcast_to(weight[pl.ds(group, 1), :], (columns, 128))
        value = (forward[:, at] + picked * by) * scale - share * rhs[:, at]
        out[:, at] = value
        total[...] = total[...] + value * value

    gather(0, first)

    @pl.loop(0, groups // 2)
    def _(step):
        gather(2 * step + 1, second)
        finish(2 * step, first)
        gather(jnp.minimum(2 * step + 2, groups - 1), first)
        finish(2 * step + 1, second)

    across = jnp.broadcast_to(jnp.sum(total[...], axis=1, keepdims=True), (columns, 128))
    squares[...] = jnp.concatenate([across] * (128 // columns), axis=0).T[0:8]


def forward_lanes(effects_all, lines, index, before, by_beta, week_square, lane_part, weight, forward, rhs, tables):
    columns, rows = rhs.shape
    height = sum(piece.shape[0] for piece in tables)
    return pl.pallas_call(
        functools.partial(forward_kernel, effects_all, lines),
        out_shape=[
            jax.ShapeDtypeStruct((columns, rows), jnp.float32),
            jax.ShapeDtypeStruct((8, 128), jnp.float32),
            jax.ShapeDtypeStruct((columns, 1), jnp.float32),
        ],
        in_specs=[SMEM] + [VMEM] * 7 + [HBM] * len(tables),
        out_specs=[VMEM] * 3,
        scratch_shapes=[
            pltpu.VMEM((height, LANES_WIDE), jnp.float32),
            pltpu.VMEM((128, LANES_WIDE), jnp.float32),
            pltpu.VMEM((128, LANES_WIDE), jnp.float32),
            pltpu.VMEM((columns, 128), jnp.float32),
            pltpu.SemaphoreType.DMA((len(tables),)),
        ],
        compiler_params=PARAMS,
        cost_estimate=takes(18),
        name="forward_lanes",
    )(index, before, by_beta, week_square, lane_part, weight, forward, rhs, *tables)


def message_kernel(lane_own, *refs):
    sources, (planes, bounds, firsts), held, arrived = refs[:7], refs[7:10], refs[10:17], refs[17]
    fitted, resid, weight, block, within, runs, signs = fetch(sources, held, arrived)
    rows = fitted.shape[0]
    planes[0:rows, :] = (block[...] * lane_own + within[...]).astype(jnp.float32)
    planes[rows : 2 * rows, :] = weight[...] * fitted[...]
    planes[2 * rows : 3 * rows, :] = weight[...] * resid[...]
    suppliers = runs.shape[1]
    across = jnp.broadcast_to(runs[...].astype(jnp.float32), (suppliers, suppliers))
    down = across.T
    at_row = lax.broadcasted_iota(jnp.int32, (suppliers, suppliers), 0)
    at_lane = lax.broadcasted_iota(jnp.int32, (suppliers, suppliers), 1)
    end_column = jnp.sum(jnp.where(at_lane <= at_row, across, 0.0), axis=1, keepdims=True)
    start_column = jnp.sum(jnp.where(at_lane < at_row, across, 0.0), axis=1, keepdims=True)
    start_row = jnp.sum(jnp.where(at_row < at_lane, down, 0.0), axis=0, keepdims=True)
    whole = (at_lane * BLOCK).astype(jnp.float32)
    first_row = jnp.sum(jnp.where(end_column <= whole, 1.0, 0.0), axis=0, keepdims=True)
    full = jnp.full((1, suppliers), rows * 128.0, jnp.float32)
    planes[3 * rows + 8 :, :] = signs[...].astype(jnp.float32)
    planes[3 * rows : 3 * rows + 8, :] = jnp.concatenate(
        [start_row, full, first_row, jnp.zeros((5, suppliers), jnp.float32)], axis=0
    )
    firsts[...] = first_row.astype(jnp.int32)
    columns = [start_column, end_column, jnp.zeros((suppliers, 6), jnp.float32)]
    bounds[0:suppliers, :] = jnp.concatenate(columns, axis=1).astype(jnp.int32)
    bounds[suppliers:, :] = jnp.full((16, 8), rows * 128, jnp.int32)


def message(lane_own, *sources):
    fitted, runs, signs = sources[0], sources[5], sources[6]
    rows = fitted.shape[0]
    suppliers = runs.shape[1]
    return pl.pallas_call(
        functools.partial(message_kernel, lane_own),
        out_shape=[
            jax.ShapeDtypeStruct((3 * rows + 8 + signs.shape[0], 128), jnp.float32),
            jax.ShapeDtypeStruct((suppliers + 16, 8), jnp.int32),
            jax.ShapeDtypeStruct((1, suppliers), jnp.int32),
        ],
        in_specs=[HBM] * 7,
        out_specs=[VMEM] * 3,
        scratch_shapes=held_for(sources),
        compiler_params=WHOLE,
        cost_estimate=takes(2),
        name="message",
    )(*sources)


def row_of(ref, start):
    pair = [ref[pl.ds(start + u, 1), :] for u in range(BLOCK // 128)]
    return jnp.concatenate(pair, axis=1)


def hot_supplier(block, bounds):
    suppliers = bounds.shape[0] - 16
    place = lax.broadcasted_iota(jnp.int32, (suppliers, BLOCK), 1) + block * BLOCK
    inside = (place >= bounds[0:suppliers, 0:1]) & (place < bounds[0:suppliers, 1:2])
    return jnp.where(inside, 1.0, 0.0).astype(jnp.bfloat16)


def hot_week(block, week, weeks):
    at = lax.broadcasted_iota(jnp.int32, (weeks, BLOCK), 0)
    same = jnp.broadcast_to(row_of(week, block * (BLOCK // 128)), (weeks, BLOCK)) == at
    return jnp.where(same, 1.0, 0.0).astype(jnp.bfloat16)


def own_sums_kernel(weeks, firsts, *refs):
    supplier, stats, by_week, fit_week, by_sign = refs[6], refs[7], *refs[-3:]
    fitted, resid, weight, week, bounds, signs = fetch(refs[:6], refs[8:14], refs[14])
    columns, suppliers = signs.shape
    blocks = fitted.shape[0] * 128 // BLOCK
    by_week[...] = jnp.zeros_like(by_week)
    fit_week[...] = jnp.zeros_like(fit_week)
    by_sign[...] = jnp.zeros_like(by_sign)
    shape = (8, BLOCK)
    place = lax.broadcasted_iota(jnp.int32, shape, 1)
    line = lax.broadcasted_iota(jnp.int32, shape, 0)

    def prepare(block):
        row = block * (BLOCK // 128)
        fit, res, by = [jnp.broadcast_to(row_of(one, row), shape) for one in (fitted, resid, weight)]
        more, less = fit + res, fit - res
        both = jnp.where(line == 0, more * more, jnp.where(line == 1, less * less, 0.0))
        both = jnp.where(line == 2, by * more, jnp.where(line == 3, by * less, both))
        return jnp.where(line == 0, by * fit, 0.0), by * res, both, hot_week(block, week, weeks)

    def group(first, block, fit, res, both, hot):
        at = place + block * BLOCK
        here = bounds[pl.ds(first, 8), :]
        inside = (at >= here[:, 0:1]) & (at < here[:, 1:2])
        left = jnp.concatenate([jnp.where(inside, res, 0.0), fit], axis=0)
        left = jnp.concatenate(split(left), axis=0)
        sums = lax.dot_general(left, hot, (((1,), (1,)), ((), ())), preferred_element_type=jnp.float32)
        mask = jnp.where(jnp.concatenate([inside, inside], axis=0), 1.0, 0.0).astype(jnp.bfloat16)
        pair = jnp.concatenate(split(both), axis=0)
        signed = lax.dot_general(mask, pair, (((1,), (1,)), ((), ())), preferred_element_type=jnp.float32)
        return sums[:16] + sums[16:], signed[:8]

    def add(first, got):
        at = pl.ds(first, 8)
        for u in range(by_week.shape[0]):
            part = got[0][:8, u * 128 : (u + 1) * 128]
            wide = slice(0, part.shape[1])
            by_week[u, at, wide] = by_week[u, at, wide] + part
        by_sign[at, 0:16] = by_sign[at, 0:16] + got[1]

    unroll = 8

    @pl.loop(0, blocks // unroll)
    def _(step):
        ready = [prepare(step * unroll + u) for u in range(unroll)]
        begin = [firsts[0, step * unroll + u] for u in range(unroll)]
        got = [group(begin[u], step * unroll + u, *ready[u]) for u in range(unroll)]
        for u in range(unroll):
            add(begin[u], got[u])
        fit_week[:, 0:weeks] = fit_week[:, 0:weeks] + sum(one[0][8:] for one in got)
        ends = begin[1:] + [firsts[0, (step + 1) * unroll]]
        more = sum((end - first) // 8 for first, end in zip(begin, ends))

        @pl.when(more > 0)
        def _():
            @pl.loop(0, unroll)
            def _(u):
                block = step * unroll + u
                start = firsts[0, block]

                @pl.loop(0, (firsts[0, block + 1] - start) // 8)
                def _(turn_at):
                    first = start + (turn_at + 1) * 8
                    fit, res, both, hot = prepare(block)
                    add(first, group(first, block, fit, res, both, hot))

    positive = signs[...] == 1
    sign = (2 * signs[...] - 1).astype(jnp.float32).astype(jnp.bfloat16)
    left = jnp.concatenate([sign, sign], axis=1)
    four = by_sign[0:suppliers, :].T
    four = four[0:8] + four[8:16]
    rows = [jnp.broadcast_to(four[u : u + 1, :], positive.shape) for u in range(4)]
    supplier[...] = jnp.where(positive, rows[2], rows[3])
    square = jnp.broadcast_to(jnp.sum(jnp.where(positive, rows[0], rows[1]), axis=1, keepdims=True), (columns, 128))
    last = lax.broadcasted_iota(jnp.int32, (columns, 128), 1) == 127
    for u in range(by_week.shape[0]):
        right = jnp.concatenate(split(by_week[u, 0:suppliers, :]), axis=0)
        part = fit_week[0:1, u * 128 : u * 128 + 128]
        part = jnp.dot(left, right, preferred_element_type=jnp.float32) + jnp.broadcast_to(part, (columns, 128))
        if u == by_week.shape[0] - 1:
            part = jnp.where(last, square, part)
        stats[u * columns : (u + 1) * columns, :] = part


def own_sums(firsts, weeks, *sources):
    columns, suppliers = sources[5].shape
    return pl.pallas_call(
        functools.partial(own_sums_kernel, weeks),
        out_shape=[
            jax.ShapeDtypeStruct((columns, suppliers), jnp.float32),
            jax.ShapeDtypeStruct((-(-weeks // 128) * columns, 128), jnp.float32),
        ],
        in_specs=[SMEM] + [HBM] * 6,
        out_specs=[VMEM] * 2,
        scratch_shapes=held_for(sources)
        + [
            pltpu.VMEM((-(-weeks // 128), suppliers + 16, 128), jnp.float32),
            pltpu.VMEM((8, -(-weeks // 128) * 128), jnp.float32),
            pltpu.VMEM((suppliers + 16, 128), jnp.float32),
        ],
        compiler_params=WHOLE,
        cost_estimate=takes(7),
        name="own_sums",
    )(firsts, *sources)


def base_kernel(*refs):
    forward, rhs_out, token = refs[8:11]
    fitted, resid, weight, week, bounds, signs, effects = fetch(refs[:7], refs[11:18], refs[18])
    columns, suppliers = signs.shape
    weeks = effects.shape[1] - suppliers
    sign = (2 * signs[...] - 1).astype(jnp.float32).astype(jnp.bfloat16)
    by_effect = jnp.concatenate(split(effects[...]), axis=0)
    blocks = fitted.shape[0] * 128 // BLOCK

    def one(block):
        row = block * (BLOCK // 128)
        by_supplier = hot_supplier(block, bounds)
        spread = jnp.dot(sign, by_supplier, preferred_element_type=jnp.float32)
        shape = (columns, BLOCK)
        at = pl.ds(pl.multiple_of(block * BLOCK, BLOCK), BLOCK)
        rhs = jnp.broadcast_to(row_of(fitted, row), shape) + spread * jnp.broadcast_to(row_of(resid, row), shape)
        rhs_out[:, at] = rhs
        hot = jnp.concatenate([by_supplier, hot_week(block, week, weeks)], axis=0)
        both = jnp.dot(by_effect, hot, preferred_element_type=jnp.float32)
        forward[:, at] = jnp.broadcast_to(row_of(weight, row), shape) * (both[:columns] + both[columns:])

    unroll = 8

    @pl.loop(0, blocks // unroll)
    def _(step):
        for u in range(unroll):
            one(step * unroll + u)

    token[...] = jnp.zeros_like(token)


def forward_base(sources, before):
    shape = jax.ShapeDtypeStruct((sources[5].shape[0], sources[0].size), jnp.float32)
    return pl.pallas_call(
        base_kernel,
        out_shape=[shape, shape, jax.ShapeDtypeStruct((8, 128), jnp.float32)],
        in_specs=[HBM] * 8,
        out_specs=[VMEM] * 3,
        scratch_shapes=held_for(sources),
        compiler_params=PARAMS,
        cost_estimate=takes(8),
        name="forward_base",
    )(*sources, before)


def near_tables(table, n_ship):
    if n_ship > 16:
        return [lax.all_gather(table, "ship", axis=0, tiled=True)]
    steps = [*range(1, n_ship // 2), *range(n_ship // 2, n_ship, 2)]
    return [table] + [swap(table, "ship", step) for step in steps]


def all_tables(near, n_ship):
    if n_ship > 16:
        return near
    tables = near[: n_ship // 2]
    for table in near[n_ship // 2 :]:
        tables += [table, swap(table, "ship", 1)]
    return tables


def effect_sums_kernel(count, residual, alpha, beta_first, supplier, entry, sums, step_out, inverse):
    columns = alpha.shape[0]
    square = jnp.broadcast_to(residual[0:1, :], (128, 128)).T[0:columns, 0:1]
    beta_next = jnp.sqrt(square / count + EPS)
    step = alpha[...] * beta_first[...] / (alpha[...] * alpha[...] + beta_next * beta_next)
    across = jnp.concatenate([jnp.broadcast_to(step, (columns, 128))] * (128 // columns), axis=0)
    step_out[...] = across.T[0:1, 0:columns]
    inverse[...] = 1.0 / beta_next
    scale = step / (alpha[...] * beta_first[...])
    rows = []
    for line in (supplier[...] * scale, entry[...] * scale):
        total = jnp.sum(line * line, axis=0, keepdims=True)
        rows += [total[:, at : at + 128] for at in range(0, line.shape[1], 128)]
    rows.append(jnp.zeros((sums.shape[0] - len(rows), 128), jnp.float32))
    sums[...] = jnp.concatenate(rows, axis=0)


def effect_sums(count, residual, alpha, beta_first, supplier, entry):
    lines = 1 + entry.shape[1] // 128
    column = jax.ShapeDtypeStruct(alpha.shape, jnp.float32)
    return pl.pallas_call(
        functools.partial(effect_sums_kernel, count),
        out_shape=[
            jax.ShapeDtypeStruct((lines // 8 * 8 + 8, 128), jnp.float32),
            jax.ShapeDtypeStruct((1, alpha.shape[0]), jnp.float32),
            column,
        ],
        in_specs=[VMEM] * 5,
        out_specs=[VMEM] * 3,
        compiler_params=SMALL,
        cost_estimate=takes(1),
        name="effect_sums",
    )(residual, alpha, beta_first, supplier, entry)


def spread_kernel(count, *refs):
    parts, supplier, lane = refs[:-2], refs[-2], refs[-1]
    total = parts[0][...]
    for part in parts[1:]:
        total = total + part[...]
    total = jnp.sqrt(total / count + EPS)
    supplier[...] = total[0:1]
    lane[...] = total[1 : 1 + lane.shape[0]]


def spreads(count, lines, parts):
    return pl.pallas_call(
        functools.partial(spread_kernel, count),
        out_shape=[jax.ShapeDtypeStruct((1, 128), jnp.float32), jax.ShapeDtypeStruct((lines, 128), jnp.float32)],
        in_specs=[VMEM] * len(parts),
        out_specs=[VMEM] * 2,
        compiler_params=SMALL,
        cost_estimate=takes(1),
        name="spreads",
    )(*parts)


def on_device(
    fitted,
    resid,
    row_weight,
    lane_block,
    lane_within,
    week_id,
    supplier_runs,
    signs,
    supplier_scale,
    lane_scale,
    week_scale,
):
    rows = fitted.shape[0]
    columns = signs.shape[0]
    n_ship = lax.axis_size("ship")
    n_boot = lax.axis_size("boot")
    me_ship = lax.axis_index("ship")
    me_boot = lax.axis_index("boot")
    lane_own = lane_scale.shape[0]
    weeks = week_scale.shape[0]
    supplier_own = supplier_scale.shape[0]
    shipments_all = rows * n_ship
    effects_all = supplier_own * n_ship + lane_own * n_ship + weeks
    ratio = effects_all / shipments_all
    share = n_ship // n_boot

    owner = lane_block[:, 0]
    square = (rows // 128, 128)
    fitted, resid, row_weight, week_id = [one.reshape(square) for one in (fitted, resid, row_weight, week_id)]

    planes, bounds, firsts = message(
        lane_own, fitted, resid, row_weight, owner.reshape(square), lane_within.reshape(square), supplier_runs, signs
    )
    got = []
    for turn in range(share):
        pairs = []
        for source in range(n_ship):
            target = (source // n_boot - turn) % share * n_boot
            for b in range(n_boot):
                pairs.append((source * n_boot + b, (target + turned(b, n_boot)) * n_boot + source % n_boot))
        got.append(lax.ppermute(planes, ("ship", "boot"), pairs))

    weeks_up = -(-weeks // 16) * 16
    held = (fitted, resid, row_weight, week_id, bounds, signs)
    supplier_part, early = own_sums(firsts, weeks_up, *held)
    got, early = lax.optimization_barrier((got, early))
    p_supplier = ratio * supplier_scale[None, :] * supplier_part
    supplier_square = jnp.sum(p_supplier * p_supplier, axis=1, keepdims=True)

    me_turn = sum(jnp.where(me_boot == b, turned(b, n_boot), 0) for b in range(n_boot))
    where = jnp.stack([me_ship * lane_own, (me_ship % n_boot) ^ me_turn]).astype(jnp.int32)
    fixed = 3 * square[0] + 8
    others = [one[fixed:] for one in got]
    blocks, step = [], 1
    for at, one in enumerate(got):
        meta = one[fixed - 8 : fixed].reshape(-1).astype(jnp.int32)
        blocks.append(lane_blocks(where, meta, one, square[0], supplier_own, lane_own))
        if step < n_boot:
            lines = step * share * columns
            back = swap(jnp.concatenate([*others, early], axis=0), "ship", step)
            others, early, step = [*others, back[:lines]], early + back[lines:], 2 * step
            if at + 1 < share:
                got[at + 1], early = lax.optimization_barrier((got[at + 1], early))
    early = sum_over(early, "ship", step)
    sums = lane_parts(where, blocks, others, columns, lane_own, supplier_own, n_boot)
    kept, later, sent = sums
    back = swap(sent, "boot", 1)
    pieces = [kept, back[:columns]]
    later = later + back[columns:]
    for step in range(1, n_boot // 2):
        pieces.append(swap(later[(step - 1) * columns : step * columns], "boot", 2 * step))
    entry, table = lane_table(ratio, lane_scale[None, :], supplier_square, pieces)
    near = near_tables(table, n_ship)

    beta_first = jnp.sqrt(early[-columns:, 127] / shipments_all + EPS)
    week_part = jnp.concatenate([early[at : at + columns] for at in range(0, early.shape[0], columns)], axis=1)
    by_beta = (1.0 / beta_first)[:, None]
    p_week = ratio * week_scale[None, :] * week_part[:, :weeks]
    week_square = jnp.sum(p_week * p_week, axis=1, keepdims=True) * by_beta * by_beta
    effects = jnp.concatenate(
        [
            p_supplier * supplier_scale[None, :],
            p_week * week_scale[None, :],
            jnp.zeros((columns, weeks_up - weeks), jnp.float32),
        ],
        axis=1,
    )

    forward, rhs, token = forward_base((*held, effects), near[min(1, len(near) - 1)][:8])
    tables = all_tables(near, n_ship)

    quarter = lane_own * columns // LANES_WIDE
    slot = owner if n_ship > 16 else owner ^ me_ship
    index = slot * (quarter + 8) + lane_within % quarter
    lane_part = (lane_within // quarter).reshape(square)
    residual, residual_sum, alpha = forward_lanes(
        effects_all, quarter, index, token, by_beta, week_square, lane_part, row_weight, forward, rhs, tables
    )
    by_both = by_beta / alpha
    v_supplier = p_supplier * by_both
    v_lane = entry * by_both
    v_week = p_week * by_both
    residual_sum = sum_over(residual_sum, "ship")
    effects, step_size, inverse = effect_sums(shipments_all, residual_sum, alpha, beta_first[:, None], p_supplier, entry)
    effects = [effects] + [swap(effects, "boot", step) for step in range(1, n_boot)]
    u_next = residual * inverse
    spread_supplier, spread_lane = spreads(columns * n_boot, lane_own // 128, effects)
    spread_supplier, spread_lane = spread_supplier.reshape(-1), spread_lane.reshape(-1)
    return (v_supplier, v_lane, v_week, u_next, step_size.reshape(-1), spread_supplier, spread_lane)


def solution(mesh):
    return jax.shard_map(
        on_device,
        mesh=mesh,
        in_specs=(
            P("ship"),
            P("ship"),
            P("ship"),
            P("ship", None),
            P("ship"),
            P("ship"),
            P("ship", None),
            P("boot", "ship"),
            P("ship"),
            P("ship"),
            P(),
        ),
        out_specs=(
            P("boot", "ship"),
            P("boot", "ship"),
            P("boot", None),
            P("boot", "ship"),
            P("boot"),
            P("ship"),
            P("ship"),
        ),
        check_vma=False,
    )
```

```python
import functools

import jax
import jax.numpy as jnp
from jax import lax
from jax.experimental import pallas as pl
from jax.experimental.pallas import tpu as pltpu
from jax.sharding import PartitionSpec as P

EPS = 1e-06
BLOCK = 256
FIRSTS = 256
SLOTS = 7
LANES_WIDE = 128
VMEM = pl.BlockSpec(memory_space=pltpu.VMEM)
SMEM = pl.BlockSpec(memory_space=pltpu.SMEM)
HBM = pl.BlockSpec(memory_space=pltpu.HBM)
PARAMS = pltpu.CompilerParams(vmem_limit_bytes=40 << 20)


WHOLE = pltpu.CompilerParams(vmem_limit_bytes=60 << 20)
SMALL = pltpu.CompilerParams(vmem_limit_bytes=8 << 20)


def takes(microseconds):
    return pl.CostEstimate(flops=0, bytes_accessed=int(microseconds * 3.6e6), transcendentals=0)


def split(value):
    high = value.astype(jnp.bfloat16)
    low = (value - high.astype(jnp.float32)).astype(jnp.bfloat16)
    return high, low


def fetch(sources, held, arrived):
    copies = [pltpu.make_async_copy(source, here, arrived.at[at]) for at, (source, here) in enumerate(zip(sources, held))]
    for copy in copies:
        copy.start()
    for copy in copies:
        copy.wait()
    return held


def held_for(sources):
    return [pltpu.VMEM(one.shape, one.dtype) for one in sources] + [pltpu.SemaphoreType.DMA((len(sources),))]


def swap(value, axis, step):
    size = lax.axis_size(axis)
    return lax.ppermute(value, axis, [(i, i ^ step) for i in range(size)])


def turned(place, size):
    bits = size.bit_length() - 1
    return sum(((place >> bit) & 1) << (bits - 1 - bit) for bit in range(bits))


def sum_over(value, axis, step=1):
    while step < lax.axis_size(axis):
        value = value + swap(value, axis, step)
        step *= 2
    return value


def lane_blocks_kernel(low_n, rows, where, meta, planes, acc, acc_fit):
    blocks = rows * 128 // BLOCK
    offset = where[0]
    shift = low_n.bit_length() - 1
    acc[...] = jnp.zeros_like(acc)
    acc_fit[...] = jnp.zeros_like(acc_fit)
    high_at = lax.broadcasted_iota(jnp.int32, (8, BLOCK), 0)
    place = lax.broadcasted_iota(jnp.int32, (8, BLOCK), 1)
    low_at = lax.broadcasted_iota(jnp.int32, (low_n, BLOCK), 0)

    def two_rows(start):
        pair = [planes[pl.ds(start + u, 1), :] for u in range(BLOCK // 128)]
        return jnp.concatenate(pair, axis=1)

    def prepare(block):
        row = block * (BLOCK // 128)
        local = two_rows(row).astype(jnp.int32) - offset
        high, low = local >> shift, local & (low_n - 1)
        match = jnp.broadcast_to(high, (8, BLOCK)) == high_at
        fit = jnp.where(match, jnp.broadcast_to(two_rows(rows + row), (8, BLOCK)), 0.0)
        res = jnp.where(match, jnp.broadcast_to(two_rows(2 * rows + row), (8, BLOCK)), 0.0)
        hot = jnp.where(jnp.broadcast_to(low, (low_n, BLOCK)) == low_at, 1.0, 0.0).astype(jnp.bfloat16)
        return fit, res, hot

    def group(first, block, fit, res, hot):
        at = place + block * BLOCK
        parts = []
        for u in range(SLOTS):
            inside = (at >= meta[first + u]) & (at < meta[first + u + 1])
            parts.append(jnp.where(inside, res, 0.0))
        left = jnp.concatenate(parts + [fit], axis=0)
        both = lax.dot_general(
            jnp.concatenate(split(left), axis=0),
            hot,
            (((1,), (1,)), ((), ())),
            preferred_element_type=jnp.float32,
        )
        return both[: 8 * SLOTS + 8] + both[8 * SLOTS + 8 :]

    def add(first, sums):
        at = pl.ds(pl.multiple_of(first * 8, 8), 8 * SLOTS)
        for u in range(low_n // 128):
            acc[u, at, :] = acc[u, at, :] + sums[: 8 * SLOTS, u * 128 : (u + 1) * 128]

    unroll = 32

    @pl.loop(0, blocks // unroll)
    def _(step):
        ready = [prepare(step * unroll + u) for u in range(unroll)]
        firsts = [meta[FIRSTS + step * unroll + u] for u in range(unroll)]
        sums = [group(firsts[u], step * unroll + u, *ready[u]) for u in range(unroll)]
        for u in range(unroll):
            add(firsts[u], sums[u])
        acc_fit[...] = acc_fit[...] + sum(one[8 * SLOTS :] for one in sums)
        ends = firsts[1:] + [meta[FIRSTS + (step + 1) * unroll]]
        more = sum((end - first) // SLOTS for first, end in zip(firsts, ends))

        @pl.when(more > 0)
        def _():
            @pl.loop(0, unroll)
            def _(u):
                block = step * unroll + u
                begin = meta[FIRSTS + block]

                @pl.loop(0, (meta[FIRSTS + block + 1] - begin) // SLOTS)
                def _(turn_at):
                    first = begin + (turn_at + 1) * SLOTS
                    fit, res, hot = prepare(block)
                    add(first, group(first, block, fit, res, hot))


def lane_blocks(where, meta, planes, rows, suppliers, own):
    low_n = max(own // 8, 128)
    return pl.pallas_call(
        functools.partial(lane_blocks_kernel, low_n, rows),
        out_shape=[
            jax.ShapeDtypeStruct((low_n // 128, (suppliers + SLOTS + 1) * 8, 128), jnp.float32),
            jax.ShapeDtypeStruct((8, low_n), jnp.float32),
        ],
        in_specs=[SMEM, SMEM, VMEM],
        out_specs=[VMEM] * 2,
        compiler_params=PARAMS,
        cost_estimate=takes(8),
        name="lane_blocks",
    )(where, meta, planes)


def lane_parts_kernel(turn_n, suppliers, share, where, *refs):
    inputs, outs, signs = refs[:-4], refs[-4:-1], refs[-1]
    accs, fits, got = inputs[:share], inputs[share : 2 * share], inputs[2 * share :]
    columns, own = outs[0].shape
    low_n = fits[0].shape[1]
    at = 0
    for piece in got:
        signs[at : at + piece.shape[0], :] = (2.0 * piece[...] - 1.0).astype(jnp.bfloat16)
        at += piece.shape[0]
    turn = where[1]
    total_fit = fits[0][...]
    for fit in fits[1:]:
        total_fit = total_fit + fit[...]
    height = share * columns
    groups = []
    for part in range(turn_n):
        here = pl.multiple_of((turn ^ turned(part, turn_n)) * height, height)
        groups.append(signs[pl.ds(here, height), :])
    lefts = []
    for step in range(share):
        left = jnp.concatenate([group[step * columns : (step + 1) * columns] for group in groups], axis=0)
        lefts.append(jnp.concatenate([left, left], axis=1))
    for high in range(-(-own // low_n)):
        total = jnp.broadcast_to(total_fit[high : high + 1, :], (turn_n * columns, low_n))
        for step in range(share):
            rows_at = pl.ds(high, suppliers, stride=8)
            wide = jnp.concatenate([accs[step][u, rows_at, :] for u in range(low_n // 128)], axis=1)
            right = jnp.concatenate(split(wide), axis=0)
            total = total + jnp.dot(lefts[step], right, preferred_element_type=jnp.float32)
        for part in range(turn_n):
            if part % 2:
                target, line = 2, (part // 2) * columns
            else:
                target, line = min(part // 2, 1), max(part // 2 - 1, 0) * columns
            value = total[part * columns : (part + 1) * columns]
            outs[target][line : line + columns, high * low_n : (high + 1) * low_n] = value


def lane_parts(where, blocks, got, columns, own, suppliers, turn_n):
    share = len(blocks)
    heights = [n * columns for n in (1, turn_n // 2 - 1, turn_n // 2)]
    return pl.pallas_call(
        functools.partial(lane_parts_kernel, turn_n, suppliers, share),
        out_shape=[jax.ShapeDtypeStruct((height, own), jnp.float32) for height in heights],
        in_specs=[SMEM] + [VMEM] * (2 * share + len(got)),
        out_specs=[VMEM] * 3,
        scratch_shapes=[pltpu.VMEM((turn_n * share * columns, suppliers), jnp.bfloat16)],
        compiler_params=PARAMS,
        cost_estimate=takes(1),
        name="lane_parts",
    )(where, *[acc for acc, _ in blocks], *[fit for _, fit in blocks], *got)


def table_kernel(ratio, scale, supplier, supplier_scale, *refs):
    parts, entries, table, supplier_out = refs[:-3], *refs[-3:]
    own = ratio * jnp.broadcast_to(supplier_scale[...], supplier.shape) * supplier[...]
    supplier_out[...] = own
    total = parts[0][...]
    for part in parts[1:]:
        total = total + part[...]
    by = jnp.broadcast_to(scale[...], total.shape)
    entry = ratio * by * total
    entries[...] = entry
    columns = total.shape[0]
    square = jnp.sum(entry * entry, axis=1, keepdims=True) + jnp.sum(own * own, axis=1, keepdims=True)
    wide = jnp.broadcast_to(square, (columns, 128))
    scaled = by * entry
    quarter = table.shape[0] - 8
    count = total.shape[1] // quarter
    stacked = jnp.concatenate([scaled[:, u * quarter : (u + 1) * quarter] for u in range(count)], axis=0)
    table[0:quarter, :] = stacked.T
    table[quarter:, :] = jnp.concatenate([wide] * (128 // columns), axis=0).T[0:8]


def lane_table(ratio, scale, supplier, supplier_scale, parts):
    columns, lanes = parts[0].shape
    quarter = lanes * columns // LANES_WIDE
    return pl.pallas_call(
        functools.partial(table_kernel, ratio),
        out_shape=[
            jax.ShapeDtypeStruct((columns, lanes), jnp.float32),
            jax.ShapeDtypeStruct((quarter + 8, LANES_WIDE), jnp.float32),
            jax.ShapeDtypeStruct(supplier.shape, jnp.float32),
        ],
        in_specs=[VMEM] * (3 + len(parts)),
        out_specs=[VMEM] * 3,
        compiler_params=SMALL,
        cost_estimate=takes(1),
        name="lane_table",
    )(scale, supplier, supplier_scale, *parts)


def forward_kernel(effects_all, lines, index, before, by_beta, week_square, lane_part, weight, forward, rhs, *refs):
    tables, (out, squares, alpha_out, table, first, second, total, landed) = refs[:-8], refs[-8:]
    columns = out.shape[0]
    copies, at = [], 0
    for place, piece in enumerate(tables):
        here = table.at[pl.ds(at, piece.shape[0])]
        copies.append(pltpu.make_async_copy(piece, here, landed.at[place]))
        at += piece.shape[0]
    for copy in copies:
        copy.start()
    for copy in copies:
        copy.wait()
    effect_square = jnp.zeros((1, 128), jnp.float32)
    for start in range(0, at, lines + 8):
        effect_square = effect_square + table[start + lines : start + lines + 1, :]
    effect_square = jnp.broadcast_to(effect_square, (128, 128)).T[0:columns]
    by = by_beta[...]
    alpha = jnp.sqrt((effect_square[:, 0:1] * by * by + week_square[...]) / effects_all + EPS)
    alpha_out[...] = alpha
    scale = jnp.broadcast_to(by / alpha, (columns, 128))
    share = jnp.broadcast_to(by * alpha, (columns, 128))
    groups = weight.shape[0]
    total[...] = jnp.zeros_like(total)

    def gather(group, store):
        for u in range(128):
            store[u : u + 1, :] = table[pl.ds(index[group * 128 + u], 1), :]

    def finish(group, store):
        turned_over = store[...].T
        part = jnp.broadcast_to(lane_part[pl.ds(group, 1), :], (columns, 128))
        picked = turned_over[0:columns]
        for u in range(1, 128 // columns):
            picked = jnp.where(part == u, turned_over[u * columns : (u + 1) * columns], picked)
        at = pl.ds(pl.multiple_of(group * 128, 128), 128)
        by = jnp.broadcast_to(weight[pl.ds(group, 1), :], (columns, 128))
        value = (forward[:, at] + picked * by) * scale - share * rhs[:, at]
        out[:, at] = value
        total[...] = total[...] + value * value

    gather(0, first)

    @pl.loop(0, groups // 2)
    def _(step):
        gather(2 * step + 1, second)
        finish(2 * step, first)
        gather(jnp.minimum(2 * step + 2, groups - 1), first)
        finish(2 * step + 1, second)

    across = jnp.broadcast_to(jnp.sum(total[...], axis=1, keepdims=True), (columns, 128))
    squares[...] = jnp.concatenate([across] * (128 // columns), axis=0).T[0:8]


def forward_lanes(effects_all, lines, index, before, by_beta, week_square, lane_part, weight, forward, rhs, tables):
    columns, rows = rhs.shape
    height = sum(piece.shape[0] for piece in tables)
    return pl.pallas_call(
        functools.partial(forward_kernel, effects_all, lines),
        out_shape=[
            jax.ShapeDtypeStruct((columns, rows), jnp.float32),
            jax.ShapeDtypeStruct((8, 128), jnp.float32),
            jax.ShapeDtypeStruct((columns, 1), jnp.float32),
        ],
        in_specs=[SMEM] + [VMEM] * 7 + [HBM] * len(tables),
        out_specs=[VMEM] * 3,
        scratch_shapes=[
            pltpu.VMEM((height, LANES_WIDE), jnp.float32),
            pltpu.VMEM((128, LANES_WIDE), jnp.float32),
            pltpu.VMEM((128, LANES_WIDE), jnp.float32),
            pltpu.VMEM((columns, 128), jnp.float32),
            pltpu.SemaphoreType.DMA((len(tables),)),
        ],
        compiler_params=PARAMS,
        cost_estimate=takes(18),
        name="forward_lanes",
    )(index, before, by_beta, week_square, lane_part, weight, forward, rhs, *tables)


def message_kernel(lane_own, *refs):
    sources, (planes, bounds, firsts), held, arrived = refs[:7], refs[7:10], refs[10:17], refs[17]
    fitted, resid, weight, block, within, runs, signs = fetch(sources, held, arrived)
    rows = fitted.shape[0]
    planes[0:rows, :] = (block[...] * lane_own + within[...]).astype(jnp.float32)
    planes[rows : 2 * rows, :] = weight[...] * fitted[...]
    planes[2 * rows : 3 * rows, :] = weight[...] * resid[...]
    suppliers = runs.shape[1]
    across = jnp.broadcast_to(runs[...].astype(jnp.float32), (suppliers, suppliers))
    down = across.T
    at_row = lax.broadcasted_iota(jnp.int32, (suppliers, suppliers), 0)
    at_lane = lax.broadcasted_iota(jnp.int32, (suppliers, suppliers), 1)
    end_column = jnp.sum(jnp.where(at_lane <= at_row, across, 0.0), axis=1, keepdims=True)
    start_column = jnp.sum(jnp.where(at_lane < at_row, across, 0.0), axis=1, keepdims=True)
    start_row = jnp.sum(jnp.where(at_row < at_lane, down, 0.0), axis=0, keepdims=True)
    whole = (at_lane * BLOCK).astype(jnp.float32)
    first_row = jnp.sum(jnp.where(end_column <= whole, 1.0, 0.0), axis=0, keepdims=True)
    full = jnp.full((1, suppliers), rows * 128.0, jnp.float32)
    planes[3 * rows + 8 :, :] = signs[...].astype(jnp.float32)
    planes[3 * rows : 3 * rows + 8, :] = jnp.concatenate(
        [start_row, full, first_row, jnp.zeros((5, suppliers), jnp.float32)], axis=0
    )
    firsts[...] = first_row.astype(jnp.int32)
    columns = [start_column, end_column, jnp.zeros((suppliers, 6), jnp.float32)]
    bounds[0:suppliers, :] = jnp.concatenate(columns, axis=1).astype(jnp.int32)
    bounds[suppliers:, :] = jnp.full((16, 8), rows * 128, jnp.int32)


def message(lane_own, *sources):
    fitted, runs, signs = sources[0], sources[5], sources[6]
    rows = fitted.shape[0]
    suppliers = runs.shape[1]
    return pl.pallas_call(
        functools.partial(message_kernel, lane_own),
        out_shape=[
            jax.ShapeDtypeStruct((3 * rows + 8 + signs.shape[0], 128), jnp.float32),
            jax.ShapeDtypeStruct((suppliers + 16, 8), jnp.int32),
            jax.ShapeDtypeStruct((1, suppliers), jnp.int32),
        ],
        in_specs=[HBM] * 7,
        out_specs=[VMEM] * 3,
        scratch_shapes=held_for(sources),
        compiler_params=WHOLE,
        cost_estimate=takes(2),
        name="message",
    )(*sources)


def row_of(ref, start):
    pair = [ref[pl.ds(start + u, 1), :] for u in range(BLOCK // 128)]
    return jnp.concatenate(pair, axis=1)


def hot_supplier(block, bounds):
    suppliers = bounds.shape[0] - 16
    place = lax.broadcasted_iota(jnp.int32, (suppliers, BLOCK), 1) + block * BLOCK
    inside = (place >= bounds[0:suppliers, 0:1]) & (place < bounds[0:suppliers, 1:2])
    return jnp.where(inside, 1.0, 0.0).astype(jnp.bfloat16)


def hot_week(block, week, weeks):
    at = lax.broadcasted_iota(jnp.int32, (weeks, BLOCK), 0)
    same = jnp.broadcast_to(row_of(week, block * (BLOCK // 128)), (weeks, BLOCK)) == at
    return jnp.where(same, 1.0, 0.0).astype(jnp.bfloat16)


def own_sums_kernel(weeks, firsts, *refs):
    supplier, stats, by_week, fit_week, by_sign = refs[6], refs[7], *refs[-3:]
    fitted, resid, weight, week, bounds, signs = fetch(refs[:6], refs[8:14], refs[14])
    columns, suppliers = signs.shape
    blocks = fitted.shape[0] * 128 // BLOCK
    by_week[...] = jnp.zeros_like(by_week)
    fit_week[...] = jnp.zeros_like(fit_week)
    by_sign[...] = jnp.zeros_like(by_sign)
    shape = (8, BLOCK)
    place = lax.broadcasted_iota(jnp.int32, shape, 1)
    line = lax.broadcasted_iota(jnp.int32, shape, 0)

    def prepare(block):
        row = block * (BLOCK // 128)
        fit, res, by = [jnp.broadcast_to(row_of(one, row), shape) for one in (fitted, resid, weight)]
        more, less = fit + res, fit - res
        both = jnp.where(line == 0, more * more, jnp.where(line == 1, less * less, 0.0))
        both = jnp.where(line == 2, by * more, jnp.where(line == 3, by * less, both))
        return jnp.where(line == 0, by * fit, 0.0), by * res, both, hot_week(block, week, weeks)

    def group(first, block, fit, res, both, hot):
        at = place + block * BLOCK
        here = bounds[pl.ds(first, 8), :]
        inside = (at >= here[:, 0:1]) & (at < here[:, 1:2])
        left = jnp.concatenate([jnp.where(inside, res, 0.0), fit], axis=0)
        left = jnp.concatenate(split(left), axis=0)
        sums = lax.dot_general(left, hot, (((1,), (1,)), ((), ())), preferred_element_type=jnp.float32)
        mask = jnp.where(jnp.concatenate([inside, inside], axis=0), 1.0, 0.0).astype(jnp.bfloat16)
        pair = jnp.concatenate(split(both), axis=0)
        signed = lax.dot_general(mask, pair, (((1,), (1,)), ((), ())), preferred_element_type=jnp.float32)
        return sums[:16] + sums[16:], signed[:8]

    def add(first, got):
        at = pl.ds(first, 8)
        for u in range(by_week.shape[0]):
            part = got[0][:8, u * 128 : (u + 1) * 128]
            wide = slice(0, part.shape[1])
            by_week[u, at, wide] = by_week[u, at, wide] + part
        by_sign[at, 0:16] = by_sign[at, 0:16] + got[1]

    unroll = 32

    @pl.loop(0, blocks // unroll)
    def _(step):
        ready = [prepare(step * unroll + u) for u in range(unroll)]
        begin = [firsts[0, step * unroll + u] for u in range(unroll)]
        got = [group(begin[u], step * unroll + u, *ready[u]) for u in range(unroll)]
        for u in range(unroll):
            add(begin[u], got[u])
        fit_week[:, 0:weeks] = fit_week[:, 0:weeks] + sum(one[0][8:] for one in got)
        ends = begin[1:] + [firsts[0, (step + 1) * unroll]]
        more = sum((end - first) // 8 for first, end in zip(begin, ends))

        @pl.when(more > 0)
        def _():
            @pl.loop(0, unroll)
            def _(u):
                block = step * unroll + u
                start = firsts[0, block]

                @pl.loop(0, (firsts[0, block + 1] - start) // 8)
                def _(turn_at):
                    first = start + (turn_at + 1) * 8
                    fit, res, both, hot = prepare(block)
                    add(first, group(first, block, fit, res, both, hot))

    positive = signs[...] == 1
    sign = (2 * signs[...] - 1).astype(jnp.float32).astype(jnp.bfloat16)
    left = jnp.concatenate([sign, sign], axis=1)
    four = by_sign[0:suppliers, :].T
    four = four[0:8] + four[8:16]
    rows = [jnp.broadcast_to(four[u : u + 1, :], positive.shape) for u in range(4)]
    supplier[...] = jnp.where(positive, rows[2], rows[3])
    square = jnp.broadcast_to(jnp.sum(jnp.where(positive, rows[0], rows[1]), axis=1, keepdims=True), (columns, 128))
    last = lax.broadcasted_iota(jnp.int32, (columns, 128), 1) == 127
    for u in range(by_week.shape[0]):
        right = jnp.concatenate(split(by_week[u, 0:suppliers, :]), axis=0)
        part = fit_week[0:1, u * 128 : u * 128 + 128]
        part = jnp.dot(left, right, preferred_element_type=jnp.float32) + jnp.broadcast_to(part, (columns, 128))
        if u == by_week.shape[0] - 1:
            part = jnp.where(last, square, part)
        stats[u * columns : (u + 1) * columns, :] = part


def own_sums(firsts, weeks, *sources):
    columns, suppliers = sources[5].shape
    return pl.pallas_call(
        functools.partial(own_sums_kernel, weeks),
        out_shape=[
            jax.ShapeDtypeStruct((columns, suppliers), jnp.float32),
            jax.ShapeDtypeStruct((-(-weeks // 128) * columns, 128), jnp.float32),
        ],
        in_specs=[SMEM] + [HBM] * 6,
        out_specs=[VMEM] * 2,
        scratch_shapes=held_for(sources)
        + [
            pltpu.VMEM((-(-weeks // 128), suppliers + 16, 128), jnp.float32),
            pltpu.VMEM((8, -(-weeks // 128) * 128), jnp.float32),
            pltpu.VMEM((suppliers + 16, 128), jnp.float32),
        ],
        compiler_params=WHOLE,
        cost_estimate=takes(7),
        name="own_sums",
    )(firsts, *sources)


def base_kernel(*refs):
    forward, rhs_out, token = refs[8:11]
    fitted, resid, weight, week, bounds, signs, effects = fetch(refs[:7], refs[11:18], refs[18])
    columns, suppliers = signs.shape
    weeks = effects.shape[1] - suppliers
    sign = (2 * signs[...] - 1).astype(jnp.float32).astype(jnp.bfloat16)
    by_effect = jnp.concatenate(split(effects[...]), axis=0)
    blocks = fitted.shape[0] * 128 // BLOCK

    def one(block):
        row = block * (BLOCK // 128)
        by_supplier = hot_supplier(block, bounds)
        spread = jnp.dot(sign, by_supplier, preferred_element_type=jnp.float32)
        shape = (columns, BLOCK)
        at = pl.ds(pl.multiple_of(block * BLOCK, BLOCK), BLOCK)
        rhs = jnp.broadcast_to(row_of(fitted, row), shape) + spread * jnp.broadcast_to(row_of(resid, row), shape)
        rhs_out[:, at] = rhs
        hot = jnp.concatenate([by_supplier, hot_week(block, week, weeks)], axis=0)
        both = jnp.dot(by_effect, hot, preferred_element_type=jnp.float32)
        forward[:, at] = jnp.broadcast_to(row_of(weight, row), shape) * (both[:columns] + both[columns:])

    unroll = 32

    @pl.loop(0, blocks // unroll)
    def _(step):
        for u in range(unroll):
            one(step * unroll + u)

    token[...] = jnp.zeros_like(token)


def forward_base(sources, before):
    shape = jax.ShapeDtypeStruct((sources[5].shape[0], sources[0].size), jnp.float32)
    return pl.pallas_call(
        base_kernel,
        out_shape=[shape, shape, jax.ShapeDtypeStruct((8, 128), jnp.float32)],
        in_specs=[HBM] * 8,
        out_specs=[VMEM] * 3,
        scratch_shapes=held_for(sources),
        compiler_params=PARAMS,
        cost_estimate=takes(8),
        name="forward_base",
    )(*sources, before)


def near_tables(table, n_ship):
    if n_ship > 16:
        return [lax.all_gather(table, "ship", axis=0, tiled=True)]
    steps = [*range(1, n_ship // 2), *range(n_ship // 2, n_ship, 2)]
    return [table] + [swap(table, "ship", step) for step in steps]


def all_tables(near, n_ship):
    if n_ship > 16:
        return near
    tables = near[: n_ship // 2]
    for table in near[n_ship // 2 :]:
        tables += [table, swap(table, "ship", 1)]
    return tables


def effect_sums_kernel(count, residual, alpha, beta_first, supplier, entry, sums, step_out, inverse):
    columns = alpha.shape[0]
    square = jnp.broadcast_to(residual[0:1, :], (128, 128)).T[0:columns, 0:1]
    beta_next = jnp.sqrt(square / count + EPS)
    step = alpha[...] * beta_first[...] / (alpha[...] * alpha[...] + beta_next * beta_next)
    across = jnp.concatenate([jnp.broadcast_to(step, (columns, 128))] * (128 // columns), axis=0)
    step_out[...] = across.T[0:1, 0:columns]
    inverse[...] = 1.0 / beta_next
    scale = step / (alpha[...] * beta_first[...])
    rows = []
    for line in (supplier[...] * scale, entry[...] * scale):
        total = jnp.sum(line * line, axis=0, keepdims=True)
        rows += [total[:, at : at + 128] for at in range(0, line.shape[1], 128)]
    rows.append(jnp.zeros((sums.shape[0] - len(rows), 128), jnp.float32))
    sums[...] = jnp.concatenate(rows, axis=0)


def effect_sums(count, residual, alpha, beta_first, supplier, entry):
    lines = 1 + entry.shape[1] // 128
    column = jax.ShapeDtypeStruct(alpha.shape, jnp.float32)
    return pl.pallas_call(
        functools.partial(effect_sums_kernel, count),
        out_shape=[
            jax.ShapeDtypeStruct((lines // 8 * 8 + 8, 128), jnp.float32),
            jax.ShapeDtypeStruct((1, alpha.shape[0]), jnp.float32),
            column,
        ],
        in_specs=[VMEM] * 5,
        out_specs=[VMEM] * 3,
        compiler_params=SMALL,
        cost_estimate=takes(1),
        name="effect_sums",
    )(residual, alpha, beta_first, supplier, entry)


def spread_kernel(count, *refs):
    parts, supplier, lane = refs[:-2], refs[-2], refs[-1]
    total = parts[0][...]
    for part in parts[1:]:
        total = total + part[...]
    total = jnp.sqrt(total / count + EPS)
    supplier[...] = total[0:1]
    lane[...] = total[1 : 1 + lane.shape[0]]


def spreads(count, lines, parts):
    return pl.pallas_call(
        functools.partial(spread_kernel, count),
        out_shape=[jax.ShapeDtypeStruct((1, 128), jnp.float32), jax.ShapeDtypeStruct((lines, 128), jnp.float32)],
        in_specs=[VMEM] * len(parts),
        out_specs=[VMEM] * 2,
        compiler_params=SMALL,
        cost_estimate=takes(1),
        name="spreads",
    )(*parts)


def on_device(
    fitted,
    resid,
    row_weight,
    lane_block,
    lane_within,
    week_id,
    supplier_runs,
    signs,
    supplier_scale,
    lane_scale,
    week_scale,
):
    rows = fitted.shape[0]
    columns = signs.shape[0]
    n_ship = lax.axis_size("ship")
    n_boot = lax.axis_size("boot")
    me_ship = lax.axis_index("ship")
    me_boot = lax.axis_index("boot")
    lane_own = lane_scale.shape[0]
    weeks = week_scale.shape[0]
    supplier_own = supplier_scale.shape[0]
    shipments_all = rows * n_ship
    effects_all = supplier_own * n_ship + lane_own * n_ship + weeks
    ratio = effects_all / shipments_all
    share = n_ship // n_boot

    owner = lane_block[:, 0]
    square = (rows // 128, 128)
    fitted, resid, row_weight, week_id = [one.reshape(square) for one in (fitted, resid, row_weight, week_id)]

    planes, bounds, firsts = message(
        lane_own, fitted, resid, row_weight, owner.reshape(square), lane_within.reshape(square), supplier_runs, signs
    )
    got = []
    for turn in range(share):
        pairs = []
        for source in range(n_ship):
            target = (source // n_boot - turn) % share * n_boot
            for b in range(n_boot):
                pairs.append((source * n_boot + b, (target + turned(b, n_boot)) * n_boot + source % n_boot))
        got.append(lax.ppermute(planes, ("ship", "boot"), pairs))

    weeks_up = -(-weeks // 16) * 16
    held = (fitted, resid, row_weight, week_id, bounds, signs)
    supplier_part, early = own_sums(firsts, weeks_up, *held)
    got, early = lax.optimization_barrier((got, early))

    me_turn = sum(jnp.where(me_boot == b, turned(b, n_boot), 0) for b in range(n_boot))
    where = jnp.stack([me_ship * lane_own, (me_ship % n_boot) ^ me_turn]).astype(jnp.int32)
    fixed = 3 * square[0] + 8
    others = [one[fixed:] for one in got]
    blocks, step = [], 1
    for at, one in enumerate(got):
        meta = one[fixed - 8 : fixed].reshape(-1).astype(jnp.int32)
        blocks.append(lane_blocks(where, meta, one, square[0], supplier_own, lane_own))
        if step < n_boot:
            lines = step * share * columns
            back = swap(jnp.concatenate([*others, early], axis=0), "ship", step)
            others, early, step = [*others, back[:lines]], early + back[lines:], 2 * step
            if at + 1 < share:
                got[at + 1], early = lax.optimization_barrier((got[at + 1], early))
    early = sum_over(early, "ship", step)
    sums = lane_parts(where, blocks, others, columns, lane_own, supplier_own, n_boot)
    kept, later, sent = sums
    back = swap(sent, "boot", 1)
    pieces = [kept, back[:columns]]
    later = later + back[columns:]
    for step in range(1, n_boot // 2):
        pieces.append(swap(later[(step - 1) * columns : step * columns], "boot", 2 * step))
    entry, table, p_supplier = lane_table(
        ratio, lane_scale[None, :], supplier_part, supplier_scale[None, :], pieces
    )
    near = near_tables(table, n_ship)

    beta_first = jnp.sqrt(early[-columns:, 127] / shipments_all + EPS)
    week_part = jnp.concatenate([early[at : at + columns] for at in range(0, early.shape[0], columns)], axis=1)
    by_beta = (1.0 / beta_first)[:, None]
    p_week = ratio * week_scale[None, :] * week_part[:, :weeks]
    week_square = jnp.sum(p_week * p_week, axis=1, keepdims=True) * by_beta * by_beta
    effects = jnp.concatenate(
        [
            p_supplier * supplier_scale[None, :],
            p_week * week_scale[None, :],
            jnp.zeros((columns, weeks_up - weeks), jnp.float32),
        ],
        axis=1,
    )

    forward, rhs, token = forward_base((*held, effects), near[min(1, len(near) - 1)][:8])
    tables = all_tables(near, n_ship)

    quarter = lane_own * columns // LANES_WIDE
    slot = owner if n_ship > 16 else owner ^ me_ship
    index = slot * (quarter + 8) + lane_within % quarter
    lane_part = (lane_within // quarter).reshape(square)
    residual, residual_sum, alpha = forward_lanes(
        effects_all, quarter, index, token, by_beta, week_square, lane_part, row_weight, forward, rhs, tables
    )
    by_both = by_beta / alpha
    v_supplier = p_supplier * by_both
    v_lane = entry * by_both
    v_week = p_week * by_both
    residual_sum = sum_over(residual_sum, "ship")
    effects, step_size, inverse = effect_sums(shipments_all, residual_sum, alpha, beta_first[:, None], p_supplier, entry)
    effects = [effects] + [swap(effects, "boot", step) for step in range(1, n_boot)]
    u_next = residual * inverse
    spread_supplier, spread_lane = spreads(columns * n_boot, lane_own // 128, effects)
    spread_supplier, spread_lane = spread_supplier.reshape(-1), spread_lane.reshape(-1)
    return (v_supplier, v_lane, v_week, u_next, step_size.reshape(-1), spread_supplier, spread_lane)


def solution(mesh):
    return jax.shard_map(
        on_device,
        mesh=mesh,
        in_specs=(
            P("ship"),
            P("ship"),
            P("ship"),
            P("ship", None),
            P("ship"),
            P("ship"),
            P("ship", None),
            P("boot", "ship"),
            P("ship"),
            P("ship"),
            P(),
        ),
        out_specs=(
            P("boot", "ship"),
            P("boot", "ship"),
            P("boot", None),
            P("boot", "ship"),
            P("boot"),
            P("ship"),
            P("ship"),
        ),
        check_vma=False,
    )
```

```python
import functools

import jax
import jax.numpy as jnp
from jax import lax
from jax.experimental import pallas as pl
from jax.experimental.pallas import tpu as pltpu
from jax.sharding import PartitionSpec as P

EPS = 1e-06
BLOCK = 256
FIRSTS = 256
SLOTS = 7
LANES_WIDE = 128
VMEM = pl.BlockSpec(memory_space=pltpu.VMEM)
SMEM = pl.BlockSpec(memory_space=pltpu.SMEM)
HBM = pl.BlockSpec(memory_space=pltpu.HBM)
PARAMS = pltpu.CompilerParams(vmem_limit_bytes=40 << 20)


WHOLE = pltpu.CompilerParams(vmem_limit_bytes=60 << 20)
SMALL = pltpu.CompilerParams(vmem_limit_bytes=8 << 20)


def takes(microseconds):
    return pl.CostEstimate(flops=0, bytes_accessed=int(microseconds * 3.6e6), transcendentals=0)


def split(value):
    high = value.astype(jnp.bfloat16)
    low = (value - high.astype(jnp.float32)).astype(jnp.bfloat16)
    return high, low


def fetch(sources, held, arrived):
    copies = [pltpu.make_async_copy(source, here, arrived.at[at]) for at, (source, here) in enumerate(zip(sources, held))]
    for copy in copies:
        copy.start()
    for copy in copies:
        copy.wait()
    return held


def held_for(sources):
    return [pltpu.VMEM(one.shape, one.dtype) for one in sources] + [pltpu.SemaphoreType.DMA((len(sources),))]


def swap(value, axis, step):
    size = lax.axis_size(axis)
    return lax.ppermute(value, axis, [(i, i ^ step) for i in range(size)])


def turned(place, size):
    bits = size.bit_length() - 1
    return sum(((place >> bit) & 1) << (bits - 1 - bit) for bit in range(bits))


def sum_over(value, axis, step=1):
    while step < lax.axis_size(axis):
        value = value + swap(value, axis, step)
        step *= 2
    return value


def lane_blocks_kernel(low_n, rows, where, meta, planes, acc, acc_fit):
    blocks = rows * 128 // BLOCK
    offset = where[0]
    shift = low_n.bit_length() - 1
    acc[...] = jnp.zeros_like(acc)
    acc_fit[...] = jnp.zeros_like(acc_fit)
    high_at = lax.broadcasted_iota(jnp.int32, (8, BLOCK), 0)
    place = lax.broadcasted_iota(jnp.int32, (8, BLOCK), 1)
    low_at = lax.broadcasted_iota(jnp.int32, (low_n, BLOCK), 0)

    def two_rows(start):
        pair = [planes[pl.ds(start + u, 1), :] for u in range(BLOCK // 128)]
        return jnp.concatenate(pair, axis=1)

    def prepare(block):
        row = block * (BLOCK // 128)
        local = two_rows(row).astype(jnp.int32) - offset
        high, low = local >> shift, local & (low_n - 1)
        match = jnp.broadcast_to(high, (8, BLOCK)) == high_at
        fit = jnp.where(match, jnp.broadcast_to(two_rows(rows + row), (8, BLOCK)), 0.0)
        res = jnp.where(match, jnp.broadcast_to(two_rows(2 * rows + row), (8, BLOCK)), 0.0)
        hot = jnp.where(jnp.broadcast_to(low, (low_n, BLOCK)) == low_at, 1.0, 0.0).astype(jnp.bfloat16)
        return fit, res, hot

    def group(first, block, fit, res, hot):
        at = place + block * BLOCK
        parts = []
        for u in range(SLOTS):
            inside = (at >= meta[first + u]) & (at < meta[first + u + 1])
            parts.append(jnp.where(inside, res, 0.0))
        left = jnp.concatenate(parts + [fit], axis=0)
        both = lax.dot_general(
            jnp.concatenate(split(left), axis=0),
            hot,
            (((1,), (1,)), ((), ())),
            preferred_element_type=jnp.float32,
        )
        return both[: 8 * SLOTS + 8] + both[8 * SLOTS + 8 :]

    def add(first, sums):
        at = pl.ds(pl.multiple_of(first * 8, 8), 8 * SLOTS)
        for u in range(low_n // 128):
            acc[u, at, :] = acc[u, at, :] + sums[: 8 * SLOTS, u * 128 : (u + 1) * 128]

    unroll = 32

    @pl.loop(0, blocks // unroll)
    def _(step):
        ready = [prepare(step * unroll + u) for u in range(unroll)]
        firsts = [meta[FIRSTS + step * unroll + u] for u in range(unroll)]
        sums = [group(firsts[u], step * unroll + u, *ready[u]) for u in range(unroll)]
        for u in range(unroll):
            add(firsts[u], sums[u])
        acc_fit[...] = acc_fit[...] + sum(one[8 * SLOTS :] for one in sums)
        ends = firsts[1:] + [meta[FIRSTS + (step + 1) * unroll]]
        more = sum((end - first) // SLOTS for first, end in zip(firsts, ends))

        @pl.when(more > 0)
        def _():
            @pl.loop(0, unroll)
            def _(u):
                block = step * unroll + u
                begin = meta[FIRSTS + block]

                @pl.loop(0, (meta[FIRSTS + block + 1] - begin) // SLOTS)
                def _(turn_at):
                    first = begin + (turn_at + 1) * SLOTS
                    fit, res, hot = prepare(block)
                    add(first, group(first, block, fit, res, hot))


def lane_blocks(where, meta, planes, rows, suppliers, own):
    low_n = max(own // 8, 128)
    return pl.pallas_call(
        functools.partial(lane_blocks_kernel, low_n, rows),
        out_shape=[
            jax.ShapeDtypeStruct((low_n // 128, (suppliers + SLOTS + 1) * 8, 128), jnp.float32),
            jax.ShapeDtypeStruct((8, low_n), jnp.float32),
        ],
        in_specs=[SMEM, SMEM, VMEM],
        out_specs=[VMEM] * 2,
        compiler_params=PARAMS,
        cost_estimate=takes(8),
        name="lane_blocks",
    )(where, meta, planes)


def lane_parts_kernel(turn_n, suppliers, share, where, *refs):
    inputs, outs, signs = refs[:-4], refs[-4:-1], refs[-1]
    accs, fits, got = inputs[:share], inputs[share : 2 * share], inputs[2 * share :]
    columns, own = outs[0].shape
    low_n = fits[0].shape[1]
    at = 0
    for piece in got:
        signs[at : at + piece.shape[0], :] = (2.0 * piece[...] - 1.0).astype(jnp.bfloat16)
        at += piece.shape[0]
    turn = where[1]
    total_fit = fits[0][...]
    for fit in fits[1:]:
        total_fit = total_fit + fit[...]
    height = share * columns
    groups = []
    for part in range(turn_n):
        here = pl.multiple_of((turn ^ turned(part, turn_n)) * height, height)
        groups.append(signs[pl.ds(here, height), :])
    lefts = []
    for step in range(share):
        left = jnp.concatenate([group[step * columns : (step + 1) * columns] for group in groups], axis=0)
        lefts.append(jnp.concatenate([left, left], axis=1))
    for high in range(-(-own // low_n)):
        total = jnp.broadcast_to(total_fit[high : high + 1, :], (turn_n * columns, low_n))
        for step in range(share):
            rows_at = pl.ds(high, suppliers, stride=8)
            wide = jnp.concatenate([accs[step][u, rows_at, :] for u in range(low_n // 128)], axis=1)
            right = jnp.concatenate(split(wide), axis=0)
            total = total + jnp.dot(lefts[step], right, preferred_element_type=jnp.float32)
        for part in range(turn_n):
            if part % 2:
                target, line = 2, (part // 2) * columns
            else:
                target, line = min(part // 2, 1), max(part // 2 - 1, 0) * columns
            value = total[part * columns : (part + 1) * columns]
            outs[target][line : line + columns, high * low_n : (high + 1) * low_n] = value


def lane_parts(where, blocks, got, columns, own, suppliers, turn_n):
    share = len(blocks)
    heights = [n * columns for n in (1, turn_n // 2 - 1, turn_n // 2)]
    return pl.pallas_call(
        functools.partial(lane_parts_kernel, turn_n, suppliers, share),
        out_shape=[jax.ShapeDtypeStruct((height, own), jnp.float32) for height in heights],
        in_specs=[SMEM] + [VMEM] * (2 * share + len(got)),
        out_specs=[VMEM] * 3,
        scratch_shapes=[pltpu.VMEM((turn_n * share * columns, suppliers), jnp.bfloat16)],
        compiler_params=PARAMS,
        cost_estimate=takes(1),
        name="lane_parts",
    )(where, *[acc for acc, _ in blocks], *[fit for _, fit in blocks], *got)


def table_kernel(ratio, scale, supplier, supplier_scale, *refs):
    parts, entries, table, supplier_out = refs[:-3], *refs[-3:]
    own = ratio * jnp.broadcast_to(supplier_scale[...], supplier.shape) * supplier[...]
    supplier_out[...] = own
    total = parts[0][...]
    for part in parts[1:]:
        total = total + part[...]
    by = jnp.broadcast_to(scale[...], total.shape)
    entry = ratio * by * total
    entries[...] = entry
    columns = total.shape[0]
    square = jnp.sum(entry * entry, axis=1, keepdims=True) + jnp.sum(own * own, axis=1, keepdims=True)
    wide = jnp.broadcast_to(square, (columns, 128))
    scaled = by * entry
    quarter = table.shape[0] - 8
    count = total.shape[1] // quarter
    stacked = jnp.concatenate([scaled[:, u * quarter : (u + 1) * quarter] for u in range(count)], axis=0)
    table[0:quarter, :] = stacked.T
    table[quarter:, :] = jnp.concatenate([wide] * (128 // columns), axis=0).T[0:8]


def lane_table(ratio, scale, supplier, supplier_scale, parts):
    columns, lanes = parts[0].shape
    quarter = lanes * columns // LANES_WIDE
    return pl.pallas_call(
        functools.partial(table_kernel, ratio),
        out_shape=[
            jax.ShapeDtypeStruct((columns, lanes), jnp.float32),
            jax.ShapeDtypeStruct((quarter + 8, LANES_WIDE), jnp.float32),
            jax.ShapeDtypeStruct(supplier.shape, jnp.float32),
        ],
        in_specs=[VMEM] * (3 + len(parts)),
        out_specs=[VMEM] * 3,
        compiler_params=SMALL,
        cost_estimate=takes(1),
        name="lane_table",
    )(scale, supplier, supplier_scale, *parts)


def forward_kernel(effects_all, lines, index, before, by_beta, week_square, lane_part, weight, forward, rhs, *refs):
    tables, (out, squares, alpha_out, table, first, second, total, landed) = refs[:-8], refs[-8:]
    columns = out.shape[0]
    copies, at = [], 0
    for place, piece in enumerate(tables):
        here = table.at[pl.ds(at, piece.shape[0])]
        copies.append(pltpu.make_async_copy(piece, here, landed.at[place]))
        at += piece.shape[0]
    for copy in copies:
        copy.start()
    for copy in copies:
        copy.wait()
    effect_square = jnp.zeros((1, 128), jnp.float32)
    for start in range(0, at, lines + 8):
        effect_square = effect_square + table[start + lines : start + lines + 1, :]
    effect_square = jnp.broadcast_to(effect_square, (128, 128)).T[0:columns]
    by = by_beta[...]
    alpha = jnp.sqrt((effect_square[:, 0:1] * by * by + week_square[...]) / effects_all + EPS)
    alpha_out[...] = alpha
    scale = jnp.broadcast_to(by / alpha, (columns, 128))
    share = jnp.broadcast_to(by * alpha, (columns, 128))
    groups = weight.shape[0]
    total[...] = jnp.zeros_like(total)

    def gather(group, store):
        for u in range(128):
            store[u : u + 1, :] = table[pl.ds(index[group * 128 + u], 1), :]

    def finish(group, store):
        turned_over = store
        part = jnp.broadcast_to(lane_part[pl.ds(group, 1), :], (columns, 128))
        picked = turned_over[0:columns]
        for u in range(1, 128 // columns):
            picked = jnp.where(part == u, turned_over[u * columns : (u + 1) * columns], picked)
        at = pl.ds(pl.multiple_of(group * 128, 128), 128)
        by = jnp.broadcast_to(weight[pl.ds(group, 1), :], (columns, 128))
        value = (forward[:, at] + picked * by) * scale - share * rhs[:, at]
        out[:, at] = value
        total[...] = total[...] + value * value

    gather(0, first)

    @pl.loop(0, groups)
    def _(group):
        turned_over = first[...].T
        gather(jnp.minimum(group + 1, groups - 1), first)
        finish(group, turned_over)

    across = jnp.broadcast_to(jnp.sum(total[...], axis=1, keepdims=True), (columns, 128))
    squares[...] = jnp.concatenate([across] * (128 // columns), axis=0).T[0:8]


def forward_lanes(effects_all, lines, index, before, by_beta, week_square, lane_part, weight, forward, rhs, tables):
    columns, rows = rhs.shape
    height = sum(piece.shape[0] for piece in tables)
    return pl.pallas_call(
        functools.partial(forward_kernel, effects_all, lines),
        out_shape=[
            jax.ShapeDtypeStruct((columns, rows), jnp.float32),
            jax.ShapeDtypeStruct((8, 128), jnp.float32),
            jax.ShapeDtypeStruct((columns, 1), jnp.float32),
        ],
        in_specs=[SMEM] + [VMEM] * 7 + [HBM] * len(tables),
        out_specs=[VMEM] * 3,
        scratch_shapes=[
            pltpu.VMEM((height, LANES_WIDE), jnp.float32),
            pltpu.VMEM((128, LANES_WIDE), jnp.float32),
            pltpu.VMEM((128, LANES_WIDE), jnp.float32),
            pltpu.VMEM((columns, 128), jnp.float32),
            pltpu.SemaphoreType.DMA((len(tables),)),
        ],
        compiler_params=PARAMS,
        cost_estimate=takes(18),
        name="forward_lanes",
    )(index, before, by_beta, week_square, lane_part, weight, forward, rhs, *tables)


def message_kernel(lane_own, *refs):
    sources, (planes, bounds, firsts), held, arrived = refs[:7], refs[7:10], refs[10:17], refs[17]
    fitted, resid, weight, block, within, runs, signs = fetch(sources, held, arrived)
    rows = fitted.shape[0]
    planes[0:rows, :] = (block[...] * lane_own + within[...]).astype(jnp.float32)
    planes[rows : 2 * rows, :] = weight[...] * fitted[...]
    planes[2 * rows : 3 * rows, :] = weight[...] * resid[...]
    suppliers = runs.shape[1]
    across = jnp.broadcast_to(runs[...].astype(jnp.float32), (suppliers, suppliers))
    down = across.T
    at_row = lax.broadcasted_iota(jnp.int32, (suppliers, suppliers), 0)
    at_lane = lax.broadcasted_iota(jnp.int32, (suppliers, suppliers), 1)
    end_column = jnp.sum(jnp.where(at_lane <= at_row, across, 0.0), axis=1, keepdims=True)
    start_column = jnp.sum(jnp.where(at_lane < at_row, across, 0.0), axis=1, keepdims=True)
    start_row = jnp.sum(jnp.where(at_row < at_lane, down, 0.0), axis=0, keepdims=True)
    whole = (at_lane * BLOCK).astype(jnp.float32)
    first_row = jnp.sum(jnp.where(end_column <= whole, 1.0, 0.0), axis=0, keepdims=True)
    full = jnp.full((1, suppliers), rows * 128.0, jnp.float32)
    planes[3 * rows + 8 :, :] = signs[...].astype(jnp.float32)
    planes[3 * rows : 3 * rows + 8, :] = jnp.concatenate(
        [start_row, full, first_row, jnp.zeros((5, suppliers), jnp.float32)], axis=0
    )
    firsts[...] = first_row.astype(jnp.int32)
    columns = [start_column, end_column, jnp.zeros((suppliers, 6), jnp.float32)]
    bounds[0:suppliers, :] = jnp.concatenate(columns, axis=1).astype(jnp.int32)
    bounds[suppliers:, :] = jnp.full((16, 8), rows * 128, jnp.int32)


def message(lane_own, *sources):
    fitted, runs, signs = sources[0], sources[5], sources[6]
    rows = fitted.shape[0]
    suppliers = runs.shape[1]
    return pl.pallas_call(
        functools.partial(message_kernel, lane_own),
        out_shape=[
            jax.ShapeDtypeStruct((3 * rows + 8 + signs.shape[0], 128), jnp.float32),
            jax.ShapeDtypeStruct((suppliers + 16, 8), jnp.int32),
            jax.ShapeDtypeStruct((1, suppliers), jnp.int32),
        ],
        in_specs=[HBM] * 7,
        out_specs=[VMEM] * 3,
        scratch_shapes=held_for(sources),
        compiler_params=WHOLE,
        cost_estimate=takes(2),
        name="message",
    )(*sources)


def row_of(ref, start):
    pair = [ref[pl.ds(start + u, 1), :] for u in range(BLOCK // 128)]
    return jnp.concatenate(pair, axis=1)


def hot_supplier(block, bounds):
    suppliers = bounds.shape[0] - 16
    place = lax.broadcasted_iota(jnp.int32, (suppliers, BLOCK), 1) + block * BLOCK
    inside = (place >= bounds[0:suppliers, 0:1]) & (place < bounds[0:suppliers, 1:2])
    return jnp.where(inside, 1.0, 0.0).astype(jnp.bfloat16)


def hot_week(block, week, weeks):
    at = lax.broadcasted_iota(jnp.int32, (weeks, BLOCK), 0)
    same = jnp.broadcast_to(row_of(week, block * (BLOCK // 128)), (weeks, BLOCK)) == at
    return jnp.where(same, 1.0, 0.0).astype(jnp.bfloat16)


def own_sums_kernel(weeks, firsts, *refs):
    supplier, stats, by_week, fit_week, by_sign = refs[6], refs[7], *refs[-3:]
    fitted, resid, weight, week, bounds, signs = fetch(refs[:6], refs[8:14], refs[14])
    columns, suppliers = signs.shape
    blocks = fitted.shape[0] * 128 // BLOCK
    by_week[...] = jnp.zeros_like(by_week)
    fit_week[...] = jnp.zeros_like(fit_week)
    by_sign[...] = jnp.zeros_like(by_sign)
    shape = (8, BLOCK)
    place = lax.broadcasted_iota(jnp.int32, shape, 1)
    line = lax.broadcasted_iota(jnp.int32, shape, 0)

    def prepare(block):
        row = block * (BLOCK // 128)
        fit, res, by = [jnp.broadcast_to(row_of(one, row), shape) for one in (fitted, resid, weight)]
        more, less = fit + res, fit - res
        both = jnp.where(line == 0, more * more, jnp.where(line == 1, less * less, 0.0))
        both = jnp.where(line == 2, by * more, jnp.where(line == 3, by * less, both))
        return jnp.where(line == 0, by * fit, 0.0), by * res, both, hot_week(block, week, weeks)

    def group(first, block, fit, res, both, hot):
        at = place + block * BLOCK
        here = bounds[pl.ds(first, 8), :]
        inside = (at >= here[:, 0:1]) & (at < here[:, 1:2])
        left = jnp.concatenate([jnp.where(inside, res, 0.0), fit], axis=0)
        left = jnp.concatenate(split(left), axis=0)
        sums = lax.dot_general(left, hot, (((1,), (1,)), ((), ())), preferred_element_type=jnp.float32)
        mask = jnp.where(jnp.concatenate([inside, inside], axis=0), 1.0, 0.0).astype(jnp.bfloat16)
        pair = jnp.concatenate(split(both), axis=0)
        signed = lax.dot_general(mask, pair, (((1,), (1,)), ((), ())), preferred_element_type=jnp.float32)
        return sums[:16] + sums[16:], signed[:8]

    def add(first, got):
        at = pl.ds(first, 8)
        for u in range(by_week.shape[0]):
            part = got[0][:8, u * 128 : (u + 1) * 128]
            wide = slice(0, part.shape[1])
            by_week[u, at, wide] = by_week[u, at, wide] + part
        by_sign[at, 0:16] = by_sign[at, 0:16] + got[1]

    unroll = 32

    @pl.loop(0, blocks // unroll)
    def _(step):
        ready = [prepare(step * unroll + u) for u in range(unroll)]
        begin = [firsts[0, step * unroll + u] for u in range(unroll)]
        got = [group(begin[u], step * unroll + u, *ready[u]) for u in range(unroll)]
        for u in range(unroll):
            add(begin[u], got[u])
        fit_week[:, 0:weeks] = fit_week[:, 0:weeks] + sum(one[0][8:] for one in got)
        ends = begin[1:] + [firsts[0, (step + 1) * unroll]]
        more = sum((end - first) // 8 for first, end in zip(begin, ends))

        @pl.when(more > 0)
        def _():
            @pl.loop(0, unroll)
            def _(u):
                block = step * unroll + u
                start = firsts[0, block]

                @pl.loop(0, (firsts[0, block + 1] - start) // 8)
                def _(turn_at):
                    first = start + (turn_at + 1) * 8
                    fit, res, both, hot = prepare(block)
                    add(first, group(first, block, fit, res, both, hot))

    positive = signs[...] == 1
    sign = (2 * signs[...] - 1).astype(jnp.float32).astype(jnp.bfloat16)
    left = jnp.concatenate([sign, sign], axis=1)
    four = by_sign[0:suppliers, :].T
    four = four[0:8] + four[8:16]
    rows = [jnp.broadcast_to(four[u : u + 1, :], positive.shape) for u in range(4)]
    supplier[...] = jnp.where(positive, rows[2], rows[3])
    square = jnp.broadcast_to(jnp.sum(jnp.where(positive, rows[0], rows[1]), axis=1, keepdims=True), (columns, 128))
    last = lax.broadcasted_iota(jnp.int32, (columns, 128), 1) == 127
    for u in range(by_week.shape[0]):
        right = jnp.concatenate(split(by_week[u, 0:suppliers, :]), axis=0)
        part = fit_week[0:1, u * 128 : u * 128 + 128]
        part = jnp.dot(left, right, preferred_element_type=jnp.float32) + jnp.broadcast_to(part, (columns, 128))
        if u == by_week.shape[0] - 1:
            part = jnp.where(last, square, part)
        stats[u * columns : (u + 1) * columns, :] = part


def own_sums(firsts, weeks, *sources):
    columns, suppliers = sources[5].shape
    return pl.pallas_call(
        functools.partial(own_sums_kernel, weeks),
        out_shape=[
            jax.ShapeDtypeStruct((columns, suppliers), jnp.float32),
            jax.ShapeDtypeStruct((-(-weeks // 128) * columns, 128), jnp.float32),
        ],
        in_specs=[SMEM] + [HBM] * 6,
        out_specs=[VMEM] * 2,
        scratch_shapes=held_for(sources)
        + [
            pltpu.VMEM((-(-weeks // 128), suppliers + 16, 128), jnp.float32),
            pltpu.VMEM((8, -(-weeks // 128) * 128), jnp.float32),
            pltpu.VMEM((suppliers + 16, 128), jnp.float32),
        ],
        compiler_params=WHOLE,
        cost_estimate=takes(7),
        name="own_sums",
    )(firsts, *sources)


def base_kernel(*refs):
    forward, rhs_out, token = refs[8:11]
    fitted, resid, weight, week, bounds, signs, effects = fetch(refs[:7], refs[11:18], refs[18])
    columns, suppliers = signs.shape
    weeks = effects.shape[1] - suppliers
    sign = (2 * signs[...] - 1).astype(jnp.float32).astype(jnp.bfloat16)
    by_effect = jnp.concatenate(split(effects[...]), axis=0)
    blocks = fitted.shape[0] * 128 // BLOCK

    def one(block):
        row = block * (BLOCK // 128)
        by_supplier = hot_supplier(block, bounds)
        spread = jnp.dot(sign, by_supplier, preferred_element_type=jnp.float32)
        shape = (columns, BLOCK)
        at = pl.ds(pl.multiple_of(block * BLOCK, BLOCK), BLOCK)
        rhs = jnp.broadcast_to(row_of(fitted, row), shape) + spread * jnp.broadcast_to(row_of(resid, row), shape)
        rhs_out[:, at] = rhs
        hot = jnp.concatenate([by_supplier, hot_week(block, week, weeks)], axis=0)
        both = jnp.dot(by_effect, hot, preferred_element_type=jnp.float32)
        forward[:, at] = jnp.broadcast_to(row_of(weight, row), shape) * (both[:columns] + both[columns:])

    unroll = 32

    @pl.loop(0, blocks // unroll)
    def _(step):
        for u in range(unroll):
            one(step * unroll + u)

    token[...] = jnp.zeros_like(token)


def forward_base(sources, before):
    shape = jax.ShapeDtypeStruct((sources[5].shape[0], sources[0].size), jnp.float32)
    return pl.pallas_call(
        base_kernel,
        out_shape=[shape, shape, jax.ShapeDtypeStruct((8, 128), jnp.float32)],
        in_specs=[HBM] * 8,
        out_specs=[VMEM] * 3,
        scratch_shapes=held_for(sources),
        compiler_params=PARAMS,
        cost_estimate=takes(8),
        name="forward_base",
    )(*sources, before)


def near_tables(table, n_ship):
    if n_ship > 16:
        return [lax.all_gather(table, "ship", axis=0, tiled=True)]
    steps = [*range(1, n_ship // 2), *range(n_ship // 2, n_ship, 2)]
    return [table] + [swap(table, "ship", step) for step in steps]


def all_tables(near, n_ship):
    if n_ship > 16:
        return near
    tables = near[: n_ship // 2]
    for table in near[n_ship // 2 :]:
        tables += [table, swap(table, "ship", 1)]
    return tables


def effect_sums_kernel(count, residual, alpha, beta_first, supplier, entry, sums, step_out, inverse):
    columns = alpha.shape[0]
    square = jnp.broadcast_to(residual[0:1, :], (128, 128)).T[0:columns, 0:1]
    beta_next = jnp.sqrt(square / count + EPS)
    step = alpha[...] * beta_first[...] / (alpha[...] * alpha[...] + beta_next * beta_next)
    across = jnp.concatenate([jnp.broadcast_to(step, (columns, 128))] * (128 // columns), axis=0)
    step_out[...] = across.T[0:1, 0:columns]
    inverse[...] = 1.0 / beta_next
    scale = step / (alpha[...] * beta_first[...])
    rows = []
    for line in (supplier[...] * scale, entry[...] * scale):
        total = jnp.sum(line * line, axis=0, keepdims=True)
        rows += [total[:, at : at + 128] for at in range(0, line.shape[1], 128)]
    rows.append(jnp.zeros((sums.shape[0] - len(rows), 128), jnp.float32))
    sums[...] = jnp.concatenate(rows, axis=0)


def effect_sums(count, residual, alpha, beta_first, supplier, entry):
    lines = 1 + entry.shape[1] // 128
    column = jax.ShapeDtypeStruct(alpha.shape, jnp.float32)
    return pl.pallas_call(
        functools.partial(effect_sums_kernel, count),
        out_shape=[
            jax.ShapeDtypeStruct((lines // 8 * 8 + 8, 128), jnp.float32),
            jax.ShapeDtypeStruct((1, alpha.shape[0]), jnp.float32),
            column,
        ],
        in_specs=[VMEM] * 5,
        out_specs=[VMEM] * 3,
        compiler_params=SMALL,
        cost_estimate=takes(1),
        name="effect_sums",
    )(residual, alpha, beta_first, supplier, entry)


def spread_kernel(count, *refs):
    parts, supplier, lane = refs[:-2], refs[-2], refs[-1]
    total = parts[0][...]
    for part in parts[1:]:
        total = total + part[...]
    total = jnp.sqrt(total / count + EPS)
    supplier[...] = total[0:1]
    lane[...] = total[1 : 1 + lane.shape[0]]


def spreads(count, lines, parts):
    return pl.pallas_call(
        functools.partial(spread_kernel, count),
        out_shape=[jax.ShapeDtypeStruct((1, 128), jnp.float32), jax.ShapeDtypeStruct((lines, 128), jnp.float32)],
        in_specs=[VMEM] * len(parts),
        out_specs=[VMEM] * 2,
        compiler_params=SMALL,
        cost_estimate=takes(1),
        name="spreads",
    )(*parts)


def on_device(
    fitted,
    resid,
    row_weight,
    lane_block,
    lane_within,
    week_id,
    supplier_runs,
    signs,
    supplier_scale,
    lane_scale,
    week_scale,
):
    rows = fitted.shape[0]
    columns = signs.shape[0]
    n_ship = lax.axis_size("ship")
    n_boot = lax.axis_size("boot")
    me_ship = lax.axis_index("ship")
    me_boot = lax.axis_index("boot")
    lane_own = lane_scale.shape[0]
    weeks = week_scale.shape[0]
    supplier_own = supplier_scale.shape[0]
    shipments_all = rows * n_ship
    effects_all = supplier_own * n_ship + lane_own * n_ship + weeks
    ratio = effects_all / shipments_all
    share = n_ship // n_boot

    owner = lane_block[:, 0]
    square = (rows // 128, 128)
    fitted, resid, row_weight, week_id = [one.reshape(square) for one in (fitted, resid, row_weight, week_id)]

    planes, bounds, firsts = message(
        lane_own, fitted, resid, row_weight, owner.reshape(square), lane_within.reshape(square), supplier_runs, signs
    )
    got = []
    for turn in range(share):
        pairs = []
        for source in range(n_ship):
            target = (source // n_boot - turn) % share * n_boot
            for b in range(n_boot):
                pairs.append((source * n_boot + b, (target + turned(b, n_boot)) * n_boot + source % n_boot))
        got.append(lax.ppermute(planes, ("ship", "boot"), pairs))

    weeks_up = -(-weeks // 16) * 16
    held = (fitted, resid, row_weight, week_id, bounds, signs)
    supplier_part, early = own_sums(firsts, weeks_up, *held)
    got, early = lax.optimization_barrier((got, early))

    me_turn = sum(jnp.where(me_boot == b, turned(b, n_boot), 0) for b in range(n_boot))
    where = jnp.stack([me_ship * lane_own, (me_ship % n_boot) ^ me_turn]).astype(jnp.int32)
    fixed = 3 * square[0] + 8
    others = [one[fixed:] for one in got]
    blocks, step = [], 1
    for at, one in enumerate(got):
        meta = one[fixed - 8 : fixed].reshape(-1).astype(jnp.int32)
        blocks.append(lane_blocks(where, meta, one, square[0], supplier_own, lane_own))
        if step < n_boot:
            lines = step * share * columns
            back = swap(jnp.concatenate([*others, early], axis=0), "ship", step)
            others, early, step = [*others, back[:lines]], early + back[lines:], 2 * step
            if at + 1 < share:
                got[at + 1], early = lax.optimization_barrier((got[at + 1], early))
    early = sum_over(early, "ship", step)
    sums = lane_parts(where, blocks, others, columns, lane_own, supplier_own, n_boot)
    kept, later, sent = sums
    back = swap(sent, "boot", 1)
    pieces = [kept, back[:columns]]
    later = later + back[columns:]
    for step in range(1, n_boot // 2):
        pieces.append(swap(later[(step - 1) * columns : step * columns], "boot", 2 * step))
    entry, table, p_supplier = lane_table(
        ratio, lane_scale[None, :], supplier_part, supplier_scale[None, :], pieces
    )
    near = near_tables(table, n_ship)

    beta_first = jnp.sqrt(early[-columns:, 127] / shipments_all + EPS)
    week_part = jnp.concatenate([early[at : at + columns] for at in range(0, early.shape[0], columns)], axis=1)
    by_beta = (1.0 / beta_first)[:, None]
    p_week = ratio * week_scale[None, :] * week_part[:, :weeks]
    week_square = jnp.sum(p_week * p_week, axis=1, keepdims=True) * by_beta * by_beta
    effects = jnp.concatenate(
        [
            p_supplier * supplier_scale[None, :],
            p_week * week_scale[None, :],
            jnp.zeros((columns, weeks_up - weeks), jnp.float32),
        ],
        axis=1,
    )

    forward, rhs, token = forward_base((*held, effects), near[min(1, len(near) - 1)][:8])
    tables = all_tables(near, n_ship)

    quarter = lane_own * columns // LANES_WIDE
    slot = owner if n_ship > 16 else owner ^ me_ship
    index = slot * (quarter + 8) + lane_within % quarter
    lane_part = (lane_within // quarter).reshape(square)
    residual, residual_sum, alpha = forward_lanes(
        effects_all, quarter, index, token, by_beta, week_square, lane_part, row_weight, forward, rhs, tables
    )
    by_both = by_beta / alpha
    v_supplier = p_supplier * by_both
    v_lane = entry * by_both
    v_week = p_week * by_both
    residual_sum = sum_over(residual_sum, "ship")
    effects, step_size, inverse = effect_sums(shipments_all, residual_sum, alpha, beta_first[:, None], p_supplier, entry)
    effects = [effects] + [swap(effects, "boot", step) for step in range(1, n_boot)]
    u_next = residual * inverse
    spread_supplier, spread_lane = spreads(columns * n_boot, lane_own // 128, effects)
    spread_supplier, spread_lane = spread_supplier.reshape(-1), spread_lane.reshape(-1)
    return (v_supplier, v_lane, v_week, u_next, step_size.reshape(-1), spread_supplier, spread_lane)


def solution(mesh):
    return jax.shard_map(
        on_device,
        mesh=mesh,
        in_specs=(
            P("ship"),
            P("ship"),
            P("ship"),
            P("ship", None),
            P("ship"),
            P("ship"),
            P("ship", None),
            P("boot", "ship"),
            P("ship"),
            P("ship"),
            P(),
        ),
        out_specs=(
            P("boot", "ship"),
            P("boot", "ship"),
            P("boot", None),
            P("boot", "ship"),
            P("boot"),
            P("ship"),
            P("ship"),
        ),
        check_vma=False,
    )
```

```python
import functools

import jax
import jax.numpy as jnp
from jax import lax
from jax.experimental import pallas as pl
from jax.experimental.pallas import tpu as pltpu
from jax.sharding import PartitionSpec as P

EPS = 1e-06
BLOCK = 256
FIRSTS = 256
SLOTS = 7
LANES_WIDE = 128
VMEM = pl.BlockSpec(memory_space=pltpu.VMEM)
SMEM = pl.BlockSpec(memory_space=pltpu.SMEM)
HBM = pl.BlockSpec(memory_space=pltpu.HBM)
PARAMS = pltpu.CompilerParams(vmem_limit_bytes=40 << 20)


WHOLE = pltpu.CompilerParams(vmem_limit_bytes=60 << 20)
SMALL = pltpu.CompilerParams(vmem_limit_bytes=8 << 20)


def takes(microseconds):
    return pl.CostEstimate(flops=0, bytes_accessed=int(microseconds * 3.6e6), transcendentals=0)


def split(value):
    high = value.astype(jnp.bfloat16)
    low = (value - high.astype(jnp.float32)).astype(jnp.bfloat16)
    return high, low


def fetch(sources, held, arrived):
    copies = [pltpu.make_async_copy(source, here, arrived.at[at]) for at, (source, here) in enumerate(zip(sources, held))]
    for copy in copies:
        copy.start()
    for copy in copies:
        copy.wait()
    return held


def held_for(sources):
    return [pltpu.VMEM(one.shape, one.dtype) for one in sources] + [pltpu.SemaphoreType.DMA((len(sources),))]


def swap(value, axis, step):
    size = lax.axis_size(axis)
    return lax.ppermute(value, axis, [(i, i ^ step) for i in range(size)])


def turned(place, size):
    bits = size.bit_length() - 1
    return sum(((place >> bit) & 1) << (bits - 1 - bit) for bit in range(bits))


def sum_over(value, axis, step=1):
    while step < lax.axis_size(axis):
        value = value + swap(value, axis, step)
        step *= 2
    return value


def lane_blocks_kernel(low_n, rows, where, meta, planes, acc, acc_fit):
    blocks = rows * 128 // BLOCK
    offset = where[0]
    shift = low_n.bit_length() - 1
    acc[...] = jnp.zeros_like(acc)
    acc_fit[...] = jnp.zeros_like(acc_fit)
    high_at = lax.broadcasted_iota(jnp.int32, (8, BLOCK), 0)
    place = lax.broadcasted_iota(jnp.int32, (8, BLOCK), 1)
    low_at = lax.broadcasted_iota(jnp.int32, (low_n, BLOCK), 0)

    def two_rows(start):
        pair = [planes[pl.ds(start + u, 1), :] for u in range(BLOCK // 128)]
        return jnp.concatenate(pair, axis=1)

    def prepare(block):
        row = block * (BLOCK // 128)
        local = two_rows(row).astype(jnp.int32) - offset
        high, low = local >> shift, local & (low_n - 1)
        match = jnp.broadcast_to(high, (8, BLOCK)) == high_at
        fit = jnp.where(match, jnp.broadcast_to(two_rows(rows + row), (8, BLOCK)), 0.0)
        res = jnp.where(match, jnp.broadcast_to(two_rows(2 * rows + row), (8, BLOCK)), 0.0)
        hot = jnp.where(jnp.broadcast_to(low, (low_n, BLOCK)) == low_at, 1.0, 0.0).astype(jnp.bfloat16)
        return fit, res, hot

    def group(first, block, fit, res, hot):
        at = place + block * BLOCK
        parts = []
        for u in range(SLOTS):
            inside = (at >= meta[first + u]) & (at < meta[first + u + 1])
            parts.append(jnp.where(inside, res, 0.0))
        left = jnp.concatenate(parts + [fit], axis=0)
        both = lax.dot_general(
            jnp.concatenate(split(left), axis=0),
            hot,
            (((1,), (1,)), ((), ())),
            preferred_element_type=jnp.float32,
        )
        return both[: 8 * SLOTS + 8] + both[8 * SLOTS + 8 :]

    def add(first, sums):
        at = pl.ds(pl.multiple_of(first * 8, 8), 8 * SLOTS)
        for u in range(low_n // 128):
            acc[u, at, :] = acc[u, at, :] + sums[: 8 * SLOTS, u * 128 : (u + 1) * 128]

    unroll = 32

    @pl.loop(0, blocks // unroll)
    def _(step):
        ready = [prepare(step * unroll + u) for u in range(unroll)]
        firsts = [meta[FIRSTS + step * unroll + u] for u in range(unroll)]
        sums = [group(firsts[u], step * unroll + u, *ready[u]) for u in range(unroll)]
        for u in range(unroll):
            add(firsts[u], sums[u])
        acc_fit[...] = acc_fit[...] + sum(one[8 * SLOTS :] for one in sums)
        ends = firsts[1:] + [meta[FIRSTS + (step + 1) * unroll]]
        more = sum((end - first) // SLOTS for first, end in zip(firsts, ends))

        @pl.when(more > 0)
        def _():
            @pl.loop(0, unroll)
            def _(u):
                block = step * unroll + u
                begin = meta[FIRSTS + block]

                @pl.loop(0, (meta[FIRSTS + block + 1] - begin) // SLOTS)
                def _(turn_at):
                    first = begin + (turn_at + 1) * SLOTS
                    fit, res, hot = prepare(block)
                    add(first, group(first, block, fit, res, hot))


def lane_blocks(where, meta, planes, rows, suppliers, own):
    low_n = max(own // 8, 128)
    return pl.pallas_call(
        functools.partial(lane_blocks_kernel, low_n, rows),
        out_shape=[
            jax.ShapeDtypeStruct((low_n // 128, (suppliers + SLOTS + 1) * 8, 128), jnp.float32),
            jax.ShapeDtypeStruct((8, low_n), jnp.float32),
        ],
        in_specs=[SMEM, SMEM, VMEM],
        out_specs=[VMEM] * 2,
        compiler_params=PARAMS,
        cost_estimate=takes(8),
        name="lane_blocks",
    )(where, meta, planes)


def lane_parts_kernel(turn_n, suppliers, share, where, *refs):
    inputs, outs, signs = refs[:-4], refs[-4:-1], refs[-1]
    accs, fits, got = inputs[:share], inputs[share : 2 * share], inputs[2 * share :]
    columns, own = outs[0].shape
    low_n = fits[0].shape[1]
    at = 0
    for piece in got:
        signs[at : at + piece.shape[0], :] = (2.0 * piece[...] - 1.0).astype(jnp.bfloat16)
        at += piece.shape[0]
    turn = where[1]
    total_fit = fits[0][...]
    for fit in fits[1:]:
        total_fit = total_fit + fit[...]
    height = share * columns
    groups = []
    for part in range(turn_n):
        here = pl.multiple_of((turn ^ turned(part, turn_n)) * height, height)
        groups.append(signs[pl.ds(here, height), :])
    lefts = []
    for step in range(share):
        left = jnp.concatenate([group[step * columns : (step + 1) * columns] for group in groups], axis=0)
        lefts.append(jnp.concatenate([left, left], axis=1))
    for high in range(-(-own // low_n)):
        total = jnp.broadcast_to(total_fit[high : high + 1, :], (turn_n * columns, low_n))
        for step in range(share):
            rows_at = pl.ds(high, suppliers, stride=8)
            wide = jnp.concatenate([accs[step][u, rows_at, :] for u in range(low_n // 128)], axis=1)
            right = jnp.concatenate(split(wide), axis=0)
            total = total + jnp.dot(lefts[step], right, preferred_element_type=jnp.float32)
        for part in range(turn_n):
            if part % 2:
                target, line = 2, (part // 2) * columns
            else:
                target, line = min(part // 2, 1), max(part // 2 - 1, 0) * columns
            value = total[part * columns : (part + 1) * columns]
            outs[target][line : line + columns, high * low_n : (high + 1) * low_n] = value


def lane_parts(where, blocks, got, columns, own, suppliers, turn_n):
    share = len(blocks)
    heights = [n * columns for n in (1, turn_n // 2 - 1, turn_n // 2)]
    return pl.pallas_call(
        functools.partial(lane_parts_kernel, turn_n, suppliers, share),
        out_shape=[jax.ShapeDtypeStruct((height, own), jnp.float32) for height in heights],
        in_specs=[SMEM] + [VMEM] * (2 * share + len(got)),
        out_specs=[VMEM] * 3,
        scratch_shapes=[pltpu.VMEM((turn_n * share * columns, suppliers), jnp.bfloat16)],
        compiler_params=PARAMS,
        cost_estimate=takes(1),
        name="lane_parts",
    )(where, *[acc for acc, _ in blocks], *[fit for _, fit in blocks], *got)


def table_kernel(ratio, scale, supplier, supplier_scale, *refs):
    parts, entries, table, supplier_out = refs[:-3], *refs[-3:]
    own = ratio * jnp.broadcast_to(supplier_scale[...], supplier.shape) * supplier[...]
    supplier_out[...] = own
    total = parts[0][...]
    for part in parts[1:]:
        total = total + part[...]
    by = jnp.broadcast_to(scale[...], total.shape)
    entry = ratio * by * total
    entries[...] = entry
    columns = total.shape[0]
    square = jnp.sum(entry * entry, axis=1, keepdims=True) + jnp.sum(own * own, axis=1, keepdims=True)
    wide = jnp.broadcast_to(square, (columns, 128))
    scaled = by * entry
    quarter = table.shape[0] - 8
    count = total.shape[1] // quarter
    stacked = jnp.concatenate([scaled[:, u * quarter : (u + 1) * quarter] for u in range(count)], axis=0)
    table[0:quarter, :] = stacked.T
    table[quarter:, :] = jnp.concatenate([wide] * (128 // columns), axis=0).T[0:8]


def lane_table(ratio, scale, supplier, supplier_scale, parts):
    columns, lanes = parts[0].shape
    quarter = lanes * columns // LANES_WIDE
    return pl.pallas_call(
        functools.partial(table_kernel, ratio),
        out_shape=[
            jax.ShapeDtypeStruct((columns, lanes), jnp.float32),
            jax.ShapeDtypeStruct((quarter + 8, LANES_WIDE), jnp.float32),
            jax.ShapeDtypeStruct(supplier.shape, jnp.float32),
        ],
        in_specs=[VMEM] * (3 + len(parts)),
        out_specs=[VMEM] * 3,
        compiler_params=SMALL,
        cost_estimate=takes(1),
        name="lane_table",
    )(scale, supplier, supplier_scale, *parts)


def forward_kernel(effects_all, lines, index, before, by_beta, week_square, lane_part, weight, forward, rhs, *refs):
    tables, (out, squares, alpha_out, table, first, second, total, landed) = refs[:-8], refs[-8:]
    columns = out.shape[0]
    copies, at = [], 0
    for place, piece in enumerate(tables):
        here = table.at[pl.ds(at, piece.shape[0])]
        copies.append(pltpu.make_async_copy(piece, here, landed.at[place]))
        at += piece.shape[0]
    for copy in copies:
        copy.start()
    for copy in copies:
        copy.wait()
    effect_square = jnp.zeros((1, 128), jnp.float32)
    for start in range(0, at, lines + 8):
        effect_square = effect_square + table[start + lines : start + lines + 1, :]
    effect_square = jnp.broadcast_to(effect_square, (128, 128)).T[0:columns]
    by = by_beta[...]
    alpha = jnp.sqrt((effect_square[:, 0:1] * by * by + week_square[...]) / effects_all + EPS)
    alpha_out[...] = alpha
    scale = jnp.broadcast_to(by / alpha, (columns, 128))
    share = jnp.broadcast_to(by * alpha, (columns, 128))
    groups = weight.shape[0]
    total[...] = jnp.zeros_like(total)

    def gather(group, store):
        for u in range(128):
            store[u : u + 1, :] = table[pl.ds(index[group * 128 + u], 1), :]

    def finish(group, store):
        turned_over = store
        part = jnp.broadcast_to(lane_part[pl.ds(group, 1), :], (columns, 128))
        picked = turned_over[0:columns]
        for u in range(1, 128 // columns):
            picked = jnp.where(part == u, turned_over[u * columns : (u + 1) * columns], picked)
        at = pl.ds(pl.multiple_of(group * 128, 128), 128)
        by = jnp.broadcast_to(weight[pl.ds(group, 1), :], (columns, 128))
        value = (forward[:, at] + picked * by) * scale - share * rhs[:, at]
        out[:, at] = value
        total[...] = total[...] + value * value

    gather(0, first)

    @pl.loop(0, groups)
    def _(group):
        finish(group, first[...].T)
        gather(jnp.minimum(group + 1, groups - 1), first)

    across = jnp.broadcast_to(jnp.sum(total[...], axis=1, keepdims=True), (columns, 128))
    squares[...] = jnp.concatenate([across] * (128 // columns), axis=0).T[0:8]


def forward_lanes(effects_all, lines, index, before, by_beta, week_square, lane_part, weight, forward, rhs, tables):
    columns, rows = rhs.shape
    height = sum(piece.shape[0] for piece in tables)
    return pl.pallas_call(
        functools.partial(forward_kernel, effects_all, lines),
        out_shape=[
            jax.ShapeDtypeStruct((columns, rows), jnp.float32),
            jax.ShapeDtypeStruct((8, 128), jnp.float32),
            jax.ShapeDtypeStruct((columns, 1), jnp.float32),
        ],
        in_specs=[SMEM] + [VMEM] * 7 + [HBM] * len(tables),
        out_specs=[VMEM] * 3,
        scratch_shapes=[
            pltpu.VMEM((height, LANES_WIDE), jnp.float32),
            pltpu.VMEM((128, LANES_WIDE), jnp.float32),
            pltpu.VMEM((128, LANES_WIDE), jnp.float32),
            pltpu.VMEM((columns, 128), jnp.float32),
            pltpu.SemaphoreType.DMA((len(tables),)),
        ],
        compiler_params=PARAMS,
        cost_estimate=takes(18),
        name="forward_lanes",
    )(index, before, by_beta, week_square, lane_part, weight, forward, rhs, *tables)


def message_kernel(lane_own, *refs):
    sources, (planes, bounds, firsts), held, arrived = refs[:7], refs[7:10], refs[10:17], refs[17]
    fitted, resid, weight, block, within, runs, signs = fetch(sources, held, arrived)
    rows = fitted.shape[0]
    planes[0:rows, :] = (block[...] * lane_own + within[...]).astype(jnp.float32)
    planes[rows : 2 * rows, :] = weight[...] * fitted[...]
    planes[2 * rows : 3 * rows, :] = weight[...] * resid[...]
    suppliers = runs.shape[1]
    across = jnp.broadcast_to(runs[...].astype(jnp.float32), (suppliers, suppliers))
    down = across.T
    at_row = lax.broadcasted_iota(jnp.int32, (suppliers, suppliers), 0)
    at_lane = lax.broadcasted_iota(jnp.int32, (suppliers, suppliers), 1)
    end_column = jnp.sum(jnp.where(at_lane <= at_row, across, 0.0), axis=1, keepdims=True)
    start_column = jnp.sum(jnp.where(at_lane < at_row, across, 0.0), axis=1, keepdims=True)
    start_row = jnp.sum(jnp.where(at_row < at_lane, down, 0.0), axis=0, keepdims=True)
    whole = (at_lane * BLOCK).astype(jnp.float32)
    first_row = jnp.sum(jnp.where(end_column <= whole, 1.0, 0.0), axis=0, keepdims=True)
    full = jnp.full((1, suppliers), rows * 128.0, jnp.float32)
    planes[3 * rows + 8 :, :] = signs[...].astype(jnp.float32)
    planes[3 * rows : 3 * rows + 8, :] = jnp.concatenate(
        [start_row, full, first_row, jnp.zeros((5, suppliers), jnp.float32)], axis=0
    )
    firsts[...] = first_row.astype(jnp.int32)
    columns = [start_column, end_column, jnp.zeros((suppliers, 6), jnp.float32)]
    bounds[0:suppliers, :] = jnp.concatenate(columns, axis=1).astype(jnp.int32)
    bounds[suppliers:, :] = jnp.full((16, 8), rows * 128, jnp.int32)


def message(lane_own, *sources):
    fitted, runs, signs = sources[0], sources[5], sources[6]
    rows = fitted.shape[0]
    suppliers = runs.shape[1]
    return pl.pallas_call(
        functools.partial(message_kernel, lane_own),
        out_shape=[
            jax.ShapeDtypeStruct((3 * rows + 8 + signs.shape[0], 128), jnp.float32),
            jax.ShapeDtypeStruct((suppliers + 16, 8), jnp.int32),
            jax.ShapeDtypeStruct((1, suppliers), jnp.int32),
        ],
        in_specs=[HBM] * 7,
        out_specs=[VMEM] * 3,
        scratch_shapes=held_for(sources),
        compiler_params=WHOLE,
        cost_estimate=takes(2),
        name="message",
    )(*sources)


def row_of(ref, start):
    pair = [ref[pl.ds(start + u, 1), :] for u in range(BLOCK // 128)]
    return jnp.concatenate(pair, axis=1)


def hot_supplier(block, bounds):
    suppliers = bounds.shape[0] - 16
    place = lax.broadcasted_iota(jnp.int32, (suppliers, BLOCK), 1) + block * BLOCK
    inside = (place >= bounds[0:suppliers, 0:1]) & (place < bounds[0:suppliers, 1:2])
    return jnp.where(inside, 1.0, 0.0).astype(jnp.bfloat16)


def hot_week(block, week, weeks):
    at = lax.broadcasted_iota(jnp.int32, (weeks, BLOCK), 0)
    same = jnp.broadcast_to(row_of(week, block * (BLOCK // 128)), (weeks, BLOCK)) == at
    return jnp.where(same, 1.0, 0.0).astype(jnp.bfloat16)


def own_sums_kernel(weeks, firsts, *refs):
    supplier, stats, by_week, fit_week, by_sign = refs[6], refs[7], *refs[-3:]
    fitted, resid, weight, week, bounds, signs = fetch(refs[:6], refs[8:14], refs[14])
    columns, suppliers = signs.shape
    blocks = fitted.shape[0] * 128 // BLOCK
    by_week[...] = jnp.zeros_like(by_week)
    fit_week[...] = jnp.zeros_like(fit_week)
    by_sign[...] = jnp.zeros_like(by_sign)
    shape = (8, BLOCK)
    place = lax.broadcasted_iota(jnp.int32, shape, 1)
    line = lax.broadcasted_iota(jnp.int32, shape, 0)

    def prepare(block):
        row = block * (BLOCK // 128)
        fit, res, by = [jnp.broadcast_to(row_of(one, row), shape) for one in (fitted, resid, weight)]
        more, less = fit + res, fit - res
        both = jnp.where(line == 0, more * more, jnp.where(line == 1, less * less, 0.0))
        both = jnp.where(line == 2, by * more, jnp.where(line == 3, by * less, both))
        return jnp.where(line == 0, by * fit, 0.0), by * res, both, hot_week(block, week, weeks)

    def group(first, block, fit, res, both, hot):
        at = place + block * BLOCK
        here = bounds[pl.ds(first, 8), :]
        inside = (at >= here[:, 0:1]) & (at < here[:, 1:2])
        left = jnp.concatenate([jnp.where(inside, res, 0.0), fit], axis=0)
        left = jnp.concatenate(split(left), axis=0)
        sums = lax.dot_general(left, hot, (((1,), (1,)), ((), ())), preferred_element_type=jnp.float32)
        mask = jnp.where(jnp.concatenate([inside, inside], axis=0), 1.0, 0.0).astype(jnp.bfloat16)
        pair = jnp.concatenate(split(both), axis=0)
        signed = lax.dot_general(mask, pair, (((1,), (1,)), ((), ())), preferred_element_type=jnp.float32)
        return sums[:16] + sums[16:], signed[:8]

    def add(first, got):
        at = pl.ds(first, 8)
        for u in range(by_week.shape[0]):
            part = got[0][:8, u * 128 : (u + 1) * 128]
            wide = slice(0, part.shape[1])
            by_week[u, at, wide] = by_week[u, at, wide] + part
        by_sign[at, 0:16] = by_sign[at, 0:16] + got[1]

    unroll = 32

    @pl.loop(0, blocks // unroll)
    def _(step):
        ready = [prepare(step * unroll + u) for u in range(unroll)]
        begin = [firsts[0, step * unroll + u] for u in range(unroll)]
        got = [group(begin[u], step * unroll + u, *ready[u]) for u in range(unroll)]
        for u in range(unroll):
            add(begin[u], got[u])
        fit_week[:, 0:weeks] = fit_week[:, 0:weeks] + sum(one[0][8:] for one in got)
        ends = begin[1:] + [firsts[0, (step + 1) * unroll]]
        more = sum((end - first) // 8 for first, end in zip(begin, ends))

        @pl.when(more > 0)
        def _():
            @pl.loop(0, unroll)
            def _(u):
                block = step * unroll + u
                start = firsts[0, block]

                @pl.loop(0, (firsts[0, block + 1] - start) // 8)
                def _(turn_at):
                    first = start + (turn_at + 1) * 8
                    fit, res, both, hot = prepare(block)
                    add(first, group(first, block, fit, res, both, hot))

    positive = signs[...] == 1
    sign = (2 * signs[...] - 1).astype(jnp.float32).astype(jnp.bfloat16)
    left = jnp.concatenate([sign, sign], axis=1)
    four = by_sign[0:suppliers, :].T
    four = four[0:8] + four[8:16]
    rows = [jnp.broadcast_to(four[u : u + 1, :], positive.shape) for u in range(4)]
    supplier[...] = jnp.where(positive, rows[2], rows[3])
    square = jnp.broadcast_to(jnp.sum(jnp.where(positive, rows[0], rows[1]), axis=1, keepdims=True), (columns, 128))
    last = lax.broadcasted_iota(jnp.int32, (columns, 128), 1) == 127
    for u in range(by_week.shape[0]):
        right = jnp.concatenate(split(by_week[u, 0:suppliers, :]), axis=0)
        part = fit_week[0:1, u * 128 : u * 128 + 128]
        part = jnp.dot(left, right, preferred_element_type=jnp.float32) + jnp.broadcast_to(part, (columns, 128))
        if u == by_week.shape[0] - 1:
            part = jnp.where(last, square, part)
        stats[u * columns : (u + 1) * columns, :] = part


def own_sums(firsts, weeks, *sources):
    columns, suppliers = sources[5].shape
    return pl.pallas_call(
        functools.partial(own_sums_kernel, weeks),
        out_shape=[
            jax.ShapeDtypeStruct((columns, suppliers), jnp.float32),
            jax.ShapeDtypeStruct((-(-weeks // 128) * columns, 128), jnp.float32),
        ],
        in_specs=[SMEM] + [HBM] * 6,
        out_specs=[VMEM] * 2,
        scratch_shapes=held_for(sources)
        + [
            pltpu.VMEM((-(-weeks // 128), suppliers + 16, 128), jnp.float32),
            pltpu.VMEM((8, -(-weeks // 128) * 128), jnp.float32),
            pltpu.VMEM((suppliers + 16, 128), jnp.float32),
        ],
        compiler_params=WHOLE,
        cost_estimate=takes(7),
        name="own_sums",
    )(firsts, *sources)


def base_kernel(*refs):
    forward, rhs_out, token = refs[8:11]
    fitted, resid, weight, week, bounds, signs, effects = fetch(refs[:7], refs[11:18], refs[18])
    columns, suppliers = signs.shape
    weeks = effects.shape[1] - suppliers
    sign = (2 * signs[...] - 1).astype(jnp.float32).astype(jnp.bfloat16)
    by_effect = jnp.concatenate(split(effects[...]), axis=0)
    blocks = fitted.shape[0] * 128 // BLOCK

    def one(block):
        row = block * (BLOCK // 128)
        by_supplier = hot_supplier(block, bounds)
        spread = jnp.dot(sign, by_supplier, preferred_element_type=jnp.float32)
        shape = (columns, BLOCK)
        at = pl.ds(pl.multiple_of(block * BLOCK, BLOCK), BLOCK)
        rhs = jnp.broadcast_to(row_of(fitted, row), shape) + spread * jnp.broadcast_to(row_of(resid, row), shape)
        rhs_out[:, at] = rhs
        hot = jnp.concatenate([by_supplier, hot_week(block, week, weeks)], axis=0)
        both = jnp.dot(by_effect, hot, preferred_element_type=jnp.float32)
        forward[:, at] = jnp.broadcast_to(row_of(weight, row), shape) * (both[:columns] + both[columns:])

    unroll = 32

    @pl.loop(0, blocks // unroll)
    def _(step):
        for u in range(unroll):
            one(step * unroll + u)

    token[...] = jnp.zeros_like(token)


def forward_base(sources, before):
    shape = jax.ShapeDtypeStruct((sources[5].shape[0], sources[0].size), jnp.float32)
    return pl.pallas_call(
        base_kernel,
        out_shape=[shape, shape, jax.ShapeDtypeStruct((8, 128), jnp.float32)],
        in_specs=[HBM] * 8,
        out_specs=[VMEM] * 3,
        scratch_shapes=held_for(sources),
        compiler_params=PARAMS,
        cost_estimate=takes(8),
        name="forward_base",
    )(*sources, before)


def near_tables(table, n_ship):
    if n_ship > 16:
        return [lax.all_gather(table, "ship", axis=0, tiled=True)]
    steps = [*range(1, n_ship // 2), *range(n_ship // 2, n_ship, 2)]
    return [table] + [swap(table, "ship", step) for step in steps]


def all_tables(near, n_ship):
    if n_ship > 16:
        return near
    tables = near[: n_ship // 2]
    for table in near[n_ship // 2 :]:
        tables += [table, swap(table, "ship", 1)]
    return tables


def effect_sums_kernel(count, residual, alpha, beta_first, supplier, entry, sums, step_out, inverse):
    columns = alpha.shape[0]
    square = jnp.broadcast_to(residual[0:1, :], (128, 128)).T[0:columns, 0:1]
    beta_next = jnp.sqrt(square / count + EPS)
    step = alpha[...] * beta_first[...] / (alpha[...] * alpha[...] + beta_next * beta_next)
    across = jnp.concatenate([jnp.broadcast_to(step, (columns, 128))] * (128 // columns), axis=0)
    step_out[...] = across.T[0:1, 0:columns]
    inverse[...] = 1.0 / beta_next
    scale = step / (alpha[...] * beta_first[...])
    rows = []
    for line in (supplier[...] * scale, entry[...] * scale):
        total = jnp.sum(line * line, axis=0, keepdims=True)
        rows += [total[:, at : at + 128] for at in range(0, line.shape[1], 128)]
    rows.append(jnp.zeros((sums.shape[0] - len(rows), 128), jnp.float32))
    sums[...] = jnp.concatenate(rows, axis=0)


def effect_sums(count, residual, alpha, beta_first, supplier, entry):
    lines = 1 + entry.shape[1] // 128
    column = jax.ShapeDtypeStruct(alpha.shape, jnp.float32)
    return pl.pallas_call(
        functools.partial(effect_sums_kernel, count),
        out_shape=[
            jax.ShapeDtypeStruct((lines // 8 * 8 + 8, 128), jnp.float32),
            jax.ShapeDtypeStruct((1, alpha.shape[0]), jnp.float32),
            column,
        ],
        in_specs=[VMEM] * 5,
        out_specs=[VMEM] * 3,
        compiler_params=SMALL,
        cost_estimate=takes(1),
        name="effect_sums",
    )(residual, alpha, beta_first, supplier, entry)


def spread_kernel(count, *refs):
    parts, supplier, lane = refs[:-2], refs[-2], refs[-1]
    total = parts[0][...]
    for part in parts[1:]:
        total = total + part[...]
    total = jnp.sqrt(total / count + EPS)
    supplier[...] = total[0:1]
    lane[...] = total[1 : 1 + lane.shape[0]]


def spreads(count, lines, parts):
    return pl.pallas_call(
        functools.partial(spread_kernel, count),
        out_shape=[jax.ShapeDtypeStruct((1, 128), jnp.float32), jax.ShapeDtypeStruct((lines, 128), jnp.float32)],
        in_specs=[VMEM] * len(parts),
        out_specs=[VMEM] * 2,
        compiler_params=SMALL,
        cost_estimate=takes(1),
        name="spreads",
    )(*parts)


def on_device(
    fitted,
    resid,
    row_weight,
    lane_block,
    lane_within,
    week_id,
    supplier_runs,
    signs,
    supplier_scale,
    lane_scale,
    week_scale,
):
    rows = fitted.shape[0]
    columns = signs.shape[0]
    n_ship = lax.axis_size("ship")
    n_boot = lax.axis_size("boot")
    me_ship = lax.axis_index("ship")
    me_boot = lax.axis_index("boot")
    lane_own = lane_scale.shape[0]
    weeks = week_scale.shape[0]
    supplier_own = supplier_scale.shape[0]
    shipments_all = rows * n_ship
    effects_all = supplier_own * n_ship + lane_own * n_ship + weeks
    ratio = effects_all / shipments_all
    share = n_ship // n_boot

    owner = lane_block[:, 0]
    square = (rows // 128, 128)
    fitted, resid, row_weight, week_id = [one.reshape(square) for one in (fitted, resid, row_weight, week_id)]

    planes, bounds, firsts = message(
        lane_own, fitted, resid, row_weight, owner.reshape(square), lane_within.reshape(square), supplier_runs, signs
    )
    got = []
    for turn in range(share):
        pairs = []
        for source in range(n_ship):
            target = (source // n_boot - turn) % share * n_boot
            for b in range(n_boot):
                pairs.append((source * n_boot + b, (target + turned(b, n_boot)) * n_boot + source % n_boot))
        got.append(lax.ppermute(planes, ("ship", "boot"), pairs))

    weeks_up = -(-weeks // 16) * 16
    held = (fitted, resid, row_weight, week_id, bounds, signs)
    supplier_part, early = own_sums(firsts, weeks_up, *held)
    got, early = lax.optimization_barrier((got, early))

    me_turn = sum(jnp.where(me_boot == b, turned(b, n_boot), 0) for b in range(n_boot))
    where = jnp.stack([me_ship * lane_own, (me_ship % n_boot) ^ me_turn]).astype(jnp.int32)
    fixed = 3 * square[0] + 8
    others = [one[fixed:] for one in got]
    blocks, step = [], 1
    for at, one in enumerate(got):
        meta = one[fixed - 8 : fixed].reshape(-1).astype(jnp.int32)
        blocks.append(lane_blocks(where, meta, one, square[0], supplier_own, lane_own))
        if step < n_boot:
            lines = step * share * columns
            back = swap(jnp.concatenate([*others, early], axis=0), "ship", step)
            others, early, step = [*others, back[:lines]], early + back[lines:], 2 * step
            if at + 1 < share:
                got[at + 1], early = lax.optimization_barrier((got[at + 1], early))
    early = sum_over(early, "ship", step)
    sums = lane_parts(where, blocks, others, columns, lane_own, supplier_own, n_boot)
    kept, later, sent = sums
    back = swap(sent, "boot", 1)
    pieces = [kept, back[:columns]]
    later = later + back[columns:]
    for step in range(1, n_boot // 2):
        pieces.append(swap(later[(step - 1) * columns : step * columns], "boot", 2 * step))
    entry, table, p_supplier = lane_table(
        ratio, lane_scale[None, :], supplier_part, supplier_scale[None, :], pieces
    )
    near = near_tables(table, n_ship)

    beta_first = jnp.sqrt(early[-columns:, 127] / shipments_all + EPS)
    week_part = jnp.concatenate([early[at : at + columns] for at in range(0, early.shape[0], columns)], axis=1)
    by_beta = (1.0 / beta_first)[:, None]
    p_week = ratio * week_scale[None, :] * week_part[:, :weeks]
    week_square = jnp.sum(p_week * p_week, axis=1, keepdims=True) * by_beta * by_beta
    effects = jnp.concatenate(
        [
            p_supplier * supplier_scale[None, :],
            p_week * week_scale[None, :],
            jnp.zeros((columns, weeks_up - weeks), jnp.float32),
        ],
        axis=1,
    )

    forward, rhs, token = forward_base((*held, effects), near[min(1, len(near) - 1)][:8])
    tables = all_tables(near, n_ship)

    quarter = lane_own * columns // LANES_WIDE
    slot = owner if n_ship > 16 else owner ^ me_ship
    index = slot * (quarter + 8) + lane_within % quarter
    lane_part = (lane_within // quarter).reshape(square)
    residual, residual_sum, alpha = forward_lanes(
        effects_all, quarter, index, token, by_beta, week_square, lane_part, row_weight, forward, rhs, tables
    )
    by_both = by_beta / alpha
    v_supplier = p_supplier * by_both
    v_lane = entry * by_both
    v_week = p_week * by_both
    residual_sum = sum_over(residual_sum, "ship")
    effects, step_size, inverse = effect_sums(shipments_all, residual_sum, alpha, beta_first[:, None], p_supplier, entry)
    effects = [effects] + [swap(effects, "boot", step) for step in range(1, n_boot)]
    u_next = residual * inverse
    spread_supplier, spread_lane = spreads(columns * n_boot, lane_own // 128, effects)
    spread_supplier, spread_lane = spread_supplier.reshape(-1), spread_lane.reshape(-1)
    return (v_supplier, v_lane, v_week, u_next, step_size.reshape(-1), spread_supplier, spread_lane)


def solution(mesh):
    return jax.shard_map(
        on_device,
        mesh=mesh,
        in_specs=(
            P("ship"),
            P("ship"),
            P("ship"),
            P("ship", None),
            P("ship"),
            P("ship"),
            P("ship", None),
            P("boot", "ship"),
            P("ship"),
            P("ship"),
            P(),
        ),
        out_specs=(
            P("boot", "ship"),
            P("boot", "ship"),
            P("boot", None),
            P("boot", "ship"),
            P("boot"),
            P("ship"),
            P("ship"),
        ),
        check_vma=False,
    )
```
